256 devices in a mesh: frm: 4 (over x), row: 16 (over z_lo, y, core), ch: 4 (over z_hi).
Axes of the slice: x: 4, y: 4, z: 8 (z_hi: 4, z_lo: 2; z = z_hi * 2 + z_lo), core: 2. Of those that a mesh axis runs over, the one named last changes fastest.
Arguments:
- latents: bfloat16 [65280, 16], P(('frm', 'row', 'ch')), may hold values from -40 to 40
- in_weight: bfloat16 [27, 16, 512], P(None, None, 'ch'), may hold values from -0.3125 to 0.3125
- in_gain: float32 [512], P('ch'), may hold values from 0.5 to 1.5
- in_shift: float32 [512], P('ch'), may hold values from -0.5 to 0.5
- mid_weight: bfloat16 [27, 512, 512], P(None, None, 'ch'), may hold values from -0.0546875 to 0.0546875
- mid_gain: float32 [512], P('ch'), may hold values from 0.5 to 1.5
- mid_shift: float32 [512], P('ch'), may hold values from -0.5 to 0.5
Outputs:
- decoded: bfloat16 [4, 96, 170, 512], P('frm', 'row', None, 'ch')
The draws below stay inside these ranges and needn't reach their ends.
All inputs are finite; a program needn't handle non-finite values.
Results may differ from the reference program's by a relative error of at most 0.015.
Values may be sent and summed in bfloat16 or wider, within the bound.
No kernel may reach another device: no remote copies, remote signals or barrier semaphores. Data moves between devices by JAX's collectives and lax.ppermute only.
A program may use at most 128 MiB of HBM per device.

```python
import jax
import jax.numpy as jnp
from jax import lax

C_LAT = 16
CH = 512
GROUPS = 32
W = 170
ROWS_DEV = 6
FRAMES = 4
H = 96


def draw_latents(key, part):
    key = jax.random.fold_in(key, 11)
    noise_key, column_key, factor_key, offset_key = jax.random.split(key, 4)
    row_total = FRAMES * H
    slab_count = row_total // ROWS_DEV
    row_pos = jnp.arange(row_total, dtype=jnp.float32) / (row_total - 1)
    column_draw = jax.random.uniform(column_key, (W,), jnp.float32)
    slab_factor = jnp.exp(jax.random.uniform(factor_key, (slab_count,), jnp.float32, -1.0, 1.0))
    slab_offset = jax.random.uniform(offset_key, (slab_count,), jnp.float32, -3.0, 3.0)
    row_factor = jnp.repeat(slab_factor, ROWS_DEV, total_repeat_length=row_total)
    row_offset = jnp.repeat(slab_offset, ROWS_DEV, total_repeat_length=row_total)
    noise_part = jnp.clip(jax.random.normal(noise_key, (row_total, W, C_LAT), jnp.float32), -4.0, 4.0)
    row_scale = jnp.power(10.0, 0.5 * row_pos)
    column_scale = jnp.power(10.0, 0.5 * column_draw)
    values = noise_part * (row_scale * row_factor)[:, None, None] * column_scale[None, :, None] + row_offset[:, None, None]
    values = jnp.clip(values, -40.0, 40.0)
    return values.reshape(row_total * W, C_LAT).astype(jnp.bfloat16)


def shard_levels(stream_key, shape, shards, smallest, largest):
    loudness = 1.0
    for position, shards_of in shards:
        steps = jax.random.uniform(jax.random.fold_in(jax.random.fold_in(stream_key, 6), position), (shards_of,), jnp.float32, smallest / len(shards), largest / len(shards))
        loudness = loudness * jnp.repeat(jnp.exp(steps), shape[position] // shards_of).reshape((-1,) + (1,) * (len(shape) - 1 - position))
    return loudness


def centred(key, shape, deviation, most, shards=(), kind=jnp.bfloat16):
    gain = shard_levels(key, shape, shards, -0.22, 0.18) if shards else 1.0
    entries = jax.random.normal(key, shape, jnp.float32) * deviation * gain
    return jnp.minimum(jnp.maximum(entries, -most), most).astype(kind)


def setup_inputs(seed: int = 0) -> dict:
    seeds = jax.random.split(jax.random.key(seed), 8)
    return {
        "latents": draw_latents(jax.random.fold_in(seeds[7], 71), 0),
        "in_weight": centred(seeds[1], (27, C_LAT, CH), (27 * C_LAT) ** -0.5, 0.3125, ((2, 4),)),
        "in_gain": jnp.clip(0.5 + 1.0 * jax.random.uniform(seeds[2], (CH,), jnp.float32) ** shard_levels(seeds[2], (CH,), ((0, 4),), -0.2, 0.2), 0.5, 1.5),
        "in_shift": jnp.clip(jax.random.uniform(seeds[3], (CH,), jnp.float32, -0.5, 0.5) * shard_levels(seeds[3], (CH,), ((0, 4),), -0.4, 0.0), -0.5, 0.5),
        "mid_weight": centred(seeds[4], (27, CH, CH), (27 * CH) ** -0.5, 0.0546875, ((2, 4),)),
        "mid_gain": jnp.clip(0.5 + 1.0 * jax.random.uniform(seeds[5], (CH,), jnp.float32) ** shard_levels(seeds[5], (CH,), ((0, 4),), -0.2, 0.2), 0.5, 1.5),
        "mid_shift": jnp.clip(jax.random.uniform(seeds[6], (CH,), jnp.float32, -0.5, 0.5) * shard_levels(seeds[6], (CH,), ((0, 4),), -0.4, 0.0), -0.5, 0.5),
    }


EPSILON = 1e-06

def causal_conv(source, weight):
    frame_count, row_count, col_count, in_chans = source.shape
    out_chans = weight.shape[2]
    padded = jnp.pad(source, ((2, 0), (1, 1), (1, 1), (0, 0)))

    def one_frame(frame_index):
        window = lax.dynamic_slice_in_dim(padded, frame_index, 3, 0)
        running = jnp.zeros((row_count * col_count, out_chans), jnp.float32)
        for frame_tap in range(3):
            for row_tap in range(3):
                for col_tap in range(3):
                    patch = window[frame_tap, row_tap:row_tap + row_count, col_tap:col_tap + col_count].reshape(-1, in_chans)
                    running = running + jnp.dot(patch, weight[9 * frame_tap + 3 * row_tap + col_tap], preferred_element_type=jnp.float32)
        return running.reshape(row_count, col_count, out_chans)
    return lax.map(one_frame, jnp.arange(frame_count, dtype=jnp.int32))

def group_norm(values, gain_vec, bias_term):
    grouped = values.reshape(-1, GROUPS, CH // GROUPS)
    centre = lax.optimization_barrier(jnp.mean(grouped, axis=(0, 2)))
    offsets = grouped - centre[None, :, None]
    spread = lax.optimization_barrier(jnp.mean(offsets * offsets, axis=(0, 2)))
    normed = offsets / jnp.sqrt(spread + EPSILON)[None, :, None]
    return normed.reshape(values.shape) * gain_vec + bias_term

def reference(latents, in_weight, in_gain, in_shift, mid_weight, mid_gain, mid_shift):
    latent_grid = latents.reshape(FRAMES, H, W, C_LAT)
    hidden = causal_conv(latent_grid, in_weight)
    activated = jax.nn.silu(group_norm(hidden, in_gain, in_shift)).astype(jnp.bfloat16)
    mixed = causal_conv(activated, mid_weight)
    return jax.nn.silu(group_norm(mixed, mid_gain, mid_shift)).astype(jnp.bfloat16)
```

```python
import jax
import jax.numpy as jnp
from jax import lax
from jax.experimental import pallas as pl
from jax.experimental.pallas import tpu as pltpu
from jax.sharding import PartitionSpec as P

CH = 512
GROUP = 16
W = 170
ROWS = 6
C_LAT = 16
FRAMES = 4
EPSILON = 1e-06

STRIDE = 176
SPAN = 8 * STRIDE
OWN = ROWS * STRIDE
TAPS = 9 * C_LAT
LEAD = 128
XLANES = 2048
WROWS = 448
CHUNKS = ((0, 384), (384, 384), (768, 384), (1152, 256))
CELLS = ROWS * W
VMEM = 48 * 1024 * 1024


def pieces3(v):
    high = lax.reduce_precision(v, 8, 7)
    mid = lax.reduce_precision(v - high, 8, 7)
    low = lax.reduce_precision(v - high - mid, 8, 7)
    return jnp.stack([high, mid, low]).astype(jnp.bfloat16)


def silu(u):
    half = 0.5 * u
    return half + half * jnp.tanh(half)


def group_mean(v):
    r = lax.broadcasted_iota(jnp.int32, (128, 128), 0) // GROUP
    c = lax.broadcasted_iota(jnp.int32, (128, 128), 1) // GROUP
    same = jnp.where(r == c, 1.0 / GROUP, 0.0).astype(jnp.float32)
    parts = [
        jnp.dot(
            v[:, i : i + 128],
            same,
            precision=lax.Precision.HIGHEST,
            preferred_element_type=jnp.float32,
        )
        for i in range(0, v.shape[1], 128)
    ]
    return parts[0] if len(parts) == 1 else jnp.concatenate(parts, axis=1)


def combine(means, squares, cells):
    n, lanes = means.shape
    mean = jnp.sum(means, axis=0, keepdims=True) / n
    off = means - mean
    var = (jnp.sum(squares, axis=0, keepdims=True) / cells + jnp.sum(off * off, axis=0, keepdims=True)) / n
    mean_g = group_mean(jnp.broadcast_to(mean, (8, lanes)))
    off_g = mean - mean_g
    var_g = group_mean(var + off_g * off_g)
    return mean_g[:1], var_g[:1]


def k1(pos_ref, g_ref, w0, w1, w2, w3, pt_ref, wall_ref, st_ref, x_ref):
    c = pos_ref[0]
    for j, w in enumerate((w0, w1, w2, w3)):
        wall_ref[lax.rem(c + j, 4)] = w[...]
    x_ref[...] = jnp.zeros_like(x_ref)
    pt_ref[: 2 * TAPS, :] = jnp.zeros((2 * TAPS, SPAN), jnp.bfloat16)

    def src(f, kind, j, lo, hi):
        return g_ref[4 * f + j, 16 * kind : 16 * kind + 16, lo:hi]

    own, nbr = 0, 1
    plan = (
        ((nbr, 2, 170, 255), (nbr, 3, 0, 85)),
        ((nbr, 3, 85, 255),),
        ((own, 0, 0, 170),),
        ((own, 0, 170, 255), (own, 1, 0, 85)),
        ((own, 1, 85, 255),),
        ((own, 2, 0, 170),),
        ((own, 2, 170, 255), (own, 3, 0, 85)),
        ((own, 3, 85, 255),),
        ((nbr, 0, 0, 170),),
        ((nbr, 0, 170, 255), (nbr, 1, 0, 85)),
    )
    for f in range(FRAMES):
        for row, parts in enumerate(plan):
            lane = LEAD + STRIDE * row
            for kind, j, lo, hi in parts:
                x_ref[16 * f : 16 * f + 16, lane : lane + hi - lo] = src(f, kind, j, lo, hi)
                lane += hi - lo
    for f in range(FRAMES):
        for b in range(3):
            for e in range(3):
                at = (f + 2) * TAPS + (3 * b + e) * 16
                lane = LEAD + STRIDE * b + e - 1
                pt_ref[at : at + 16, :] = x_ref[16 * f : 16 * f + 16, lane : lane + SPAN]

    weight = jnp.concatenate([wall_ref[j, :432, :] for j in range(4)], axis=1)

    def hidden(g, lo, size):
        at = pl.multiple_of(g * TAPS, 16)
        return lax.dot_general(
            pt_ref[pl.ds(at, 3 * TAPS), lo : lo + size],
            weight,
            (((0,), (0,)), ((), ())),
            preferred_element_type=jnp.float32,
        )

    def valid(lo, size):
        at = lo + lax.broadcasted_iota(jnp.int32, (size, 128), 0)
        ok = (at >= STRIDE) & (at < STRIDE + OWN)
        for row in range(1, 7):
            gap = STRIDE * row + W
            if lo < gap + STRIDE - W and gap < lo + size:
                ok = ok & ((at < gap) | (at >= gap + STRIDE - W))
        return jnp.concatenate([ok] * 4, axis=1)

    first = hidden(0, 256, 128)
    pilot = jnp.sum(jnp.where(valid(256, 128), first, 0.0), axis=0, keepdims=True) * (1.0 / 122)

    def frame(g, carry):
        s1, s2 = carry
        for lo, size in CHUNKS:
            h = hidden(g, lo, size)
            d = jnp.where(valid(lo, size), h - pilot, 0.0)
            d = d.reshape(size // 8, 8, CH)
            s1 = s1 + jnp.sum(d, axis=0)
            s2 = s2 + jnp.sum(d * d, axis=0)
        return s1, s2

    zero = jnp.zeros((8, CH), jnp.float32)
    s1, s2 = lax.fori_loop(0, FRAMES, frame, (zero, zero))
    n = FRAMES * CELLS
    s1 = jnp.sum(s1, axis=0, keepdims=True)
    s2 = jnp.sum(s2, axis=0, keepdims=True)
    d = s1 / n
    st_ref[:, 0:1, :] = jnp.broadcast_to((pilot + d)[None], (16, 1, CH))
    st_ref[:, 1:2, :] = jnp.broadcast_to((s2 - s1 * d)[None], (16, 1, CH))


def k2(pos_ref, pt_ref, wall_ref, st_ref, w2_hbm, mix_ref, so_ref, a_ref, w2_ref, y_ref, sem):
    copy = pltpu.make_async_copy(w2_hbm, w2_ref, sem)
    copy.start()
    f, top, bottom = pos_ref[1], pos_ref[2], pos_ref[3]
    weight = jnp.concatenate([wall_ref[j, :432, :] for j in range(4)], axis=1)
    extra = jnp.concatenate([wall_ref[j, 432:, :] for j in range(4)], axis=1).astype(jnp.float32)
    gain = extra[0:1] + extra[1:2] + extra[2:3]
    shift = extra[3:4] + extra[4:5] + extra[5:6]
    mean, var = combine(st_ref[:, 0, :], st_ref[:, 1, :], FRAMES * CELLS)
    scale = lax.rsqrt(var + EPSILON) * gain

    a_ref[0:16, :] = jnp.zeros((16, 3 * CH), jnp.bfloat16)
    a_ref[16 + SPAN :, :] = jnp.zeros((16, 3 * CH), jnp.bfloat16)
    for k in range(3):
        g = f - 2 + k

        @pl.when(g >= 0)
        def _():
            at = pl.multiple_of(g * TAPS, 16)
            for lo, size in CHUNKS:
                h = lax.dot_general(
                    pt_ref[pl.ds(at, 3 * TAPS), lo : lo + size],
                    weight,
                    (((0,), (0,)), ((), ())),
                    preferred_element_type=jnp.float32,
                )
                u = (h - mean) * scale + shift
                a_ref[16 + lo : 16 + lo + size, k * CH : (k + 1) * CH] = silu(u).astype(jnp.bfloat16)

        @pl.when(g < 0)
        def _():
            a_ref[16 : 16 + SPAN, k * CH : (k + 1) * CH] = jnp.zeros((SPAN, CH), jnp.bfloat16)

    keep = lax.broadcasted_iota(jnp.int32, (16, 3 * CH), 0) < 10
    for row in range(8):
        at = 16 + STRIDE * row + 160
        a_ref[at : at + 16, :] = jnp.where(keep, a_ref[at : at + 16, :], 0).astype(jnp.bfloat16)

    @pl.when(top == 1)
    def _():
        a_ref[16 : 16 + STRIDE, :] = jnp.zeros((STRIDE, 3 * CH), jnp.bfloat16)

    @pl.when(bottom == 1)
    def _():
        a_ref[16 + 7 * STRIDE : 16 + SPAN, :] = jnp.zeros((STRIDE, 3 * CH), jnp.bfloat16)

    copy.wait()

    def taps(b, e):
        return jnp.concatenate([w2_ref[9 * a + 3 * b + e] for a in range(3)], axis=0)

    def product(start, step, steps, kernel):
        lanes = kernel.shape[1]

        def one(i, _):
            at = pl.multiple_of(i * step, 16)
            y_ref[pl.ds(at, step), :lanes] = jnp.dot(
                a_ref[pl.ds(start + at, step), :], kernel, preferred_element_type=jnp.float32
            )
            return 0

        lax.fori_loop(0, steps, one, 0)

    for b in range(3):
        product(STRIDE * b, 272, 4, jnp.concatenate([taps(b, 0), taps(b, 2)], axis=1))
        part = y_ref[15 : 15 + OWN, :128] + y_ref[17 : 17 + OWN, 128:]
        mix_ref[...] = part if b == 0 else mix_ref[...] + part
    product(16, 352, 4, jnp.concatenate([taps(0, 1), taps(2, 1)], axis=1))
    mix_ref[...] += y_ref[0:OWN, :128] + y_ref[2 * STRIDE : 2 * STRIDE + OWN, 128:]
    product(16 + STRIDE, 352, 3, taps(1, 1))
    v = (mix_ref[...] + y_ref[0:OWN, :128]).reshape(ROWS, STRIDE, 128)
    mix_ref[...] = v.reshape(OWN, 128)
    ok = lax.broadcasted_iota(jnp.int32, (ROWS, STRIDE, 128), 1) < W
    total = jnp.sum(jnp.sum(jnp.where(ok, v, 0.0), axis=0), axis=0, keepdims=True)
    centre = total / CELLS
    off = jnp.where(ok, v - centre[None], 0.0)
    squares = jnp.sum(jnp.sum(off * off, axis=0), axis=0, keepdims=True)
    so_ref[:, 0:1, :] = jnp.broadcast_to(centre[None], (64, 1, 128))
    so_ref[:, 1:2, :] = jnp.broadcast_to(squares[None], (64, 1, 128))


def k3(mix_ref, st_ref, gain_ref, shift_ref, out_ref):
    mean, var = combine(st_ref[:, 0, :], st_ref[:, 1, :], CELLS)
    scale = lax.rsqrt(var + EPSILON) * gain_ref[...]
    for row in range(ROWS):
        v = mix_ref[STRIDE * row : STRIDE * (row + 1), :]
        u = silu((v - mean) * scale + shift_ref[...])
        out_ref[0, row] = u[:W].astype(jnp.bfloat16)


def shape(dims, kind):
    return jax.ShapeDtypeStruct(dims, kind)


SMEM = pl.BlockSpec(memory_space=pltpu.SMEM)
INVMEM = pl.BlockSpec(memory_space=pltpu.VMEM)


def call_k1(pos, g, ws):
    return pl.pallas_call(
        k1,
        out_shape=(
            shape((6 * TAPS, SPAN), jnp.bfloat16),
            shape((4, WROWS, 128), jnp.bfloat16),
            shape((16, 2, CH), jnp.float32),
        ),
        in_specs=[SMEM] + [INVMEM] * 5,
        out_specs=(INVMEM,) * 3,
        scratch_shapes=[pltpu.VMEM((16 * FRAMES, XLANES), jnp.bfloat16)],
        compiler_params=pltpu.CompilerParams(vmem_limit_bytes=VMEM),
    )(pos, g, *ws)


def call_k2(pos, pt, wall, st, w2):
    return pl.pallas_call(
        k2,
        out_shape=(shape((OWN, 128), jnp.float32), shape((64, 2, 128), jnp.float32)),
        in_specs=[SMEM] + [INVMEM] * 3 + [pl.BlockSpec(memory_space=pl.ANY)],
        out_specs=(INVMEM,) * 2,
        scratch_shapes=[
            pltpu.VMEM((SPAN + 32, 3 * CH), jnp.bfloat16),
            pltpu.VMEM((27, CH, 128), jnp.bfloat16),
            pltpu.VMEM((SPAN, 256), jnp.float32),
            pltpu.SemaphoreType.DMA,
        ],
        compiler_params=pltpu.CompilerParams(vmem_limit_bytes=VMEM),
    )(pos, pt, wall, st, w2)


def call_k3(mix, st, gain, bias):
    return pl.pallas_call(
        k3,
        out_shape=shape((1, ROWS, W, 128), jnp.bfloat16),
        in_specs=[INVMEM] * 4,
        out_specs=INVMEM,
        compiler_params=pltpu.CompilerParams(vmem_limit_bytes=VMEM),
    )(mix, st, gain, bias)


def per_device(latents, in_weight, in_gain, in_shift, mid_weight, mid_gain, mid_shift):
    f, r, c = (lax.axis_index(axis) for axis in ("frm", "row", "ch"))
    pos = jnp.stack([c, f, r == 0, r == 15]).astype(jnp.int32)
    nbrs = [(4 * (i + 1) + j, 4 * i + j) for i in range(15) for j in (0, 1)]
    nbrs += [(4 * i + j, 4 * (i + 1) + j) for i in range(15) for j in (2, 3)]
    tokens = latents.T
    nbr = lax.ppermute(tokens, ("row", "ch"), nbrs)
    held = jnp.concatenate(
        [
            in_weight.reshape(27 * C_LAT, 128),
            pieces3(in_gain),
            pieces3(in_shift),
            jnp.zeros((WROWS - 438, 128), jnp.bfloat16),
        ]
    )
    ws = [held] + [lax.ppermute(held, "ch", [((i + k) % 4, i) for i in range(4)]) for k in (1, 2, 3)]
    payload = jnp.concatenate([tokens, nbr], axis=0)
    g = lax.all_to_all(jnp.broadcast_to(payload[None], (16, 32, 255)), ("frm", "ch"), 0, 0)
    pt, wall, st = call_k1(pos, g, ws)
    st = lax.all_to_all(st, "row", 0, 0)
    mix, st = call_k2(pos, pt, wall, st, mid_weight)
    st = lax.all_to_all(st, ("frm", "row"), 0, 0)
    return call_k3(mix, st, mid_gain.reshape(1, 128), mid_shift.reshape(1, 128))


def solution(mesh):
    return jax.shard_map(
        per_device,
        mesh=mesh,
        in_specs=(
            P(("frm", "row", "ch"), None),
            P(None, None, "ch"),
            P("ch"),
            P("ch"),
            P(None, None, "ch"),
            P("ch"),
            P("ch"),
        ),
        out_specs=P("frm", "row", None, "ch"),
        check_vma=False,
    )
```

```python
import jax
import jax.numpy as jnp
from jax import lax
from jax.experimental import pallas as pl
from jax.experimental.pallas import tpu as pltpu
from jax.sharding import PartitionSpec as P

CH = 512
GROUP = 16
W = 170
ROWS = 6
C_LAT = 16
FRAMES = 4
EPSILON = 1e-06

STRIDE = 176
SPAN = 8 * STRIDE
OWN = ROWS * STRIDE
TAPS = 9 * C_LAT
LEAD = 128
XLANES = 2048
K1_CHUNKS = ((128, 384), (512, 384), (896, 384))
CHUNKS = ((0, 384), (384, 384), (768, 384), (1152, 256))
CELLS = ROWS * W
TAPROWS = 27 * C_LAT
HELD = 448
PIECE = 64
PIECES = tuple(i * 24 // 7 * 16 for i in range(8))
VMEM = 48 * 1024 * 1024


def silu_of_twice(half):
    return half + half * jnp.tanh(half)


def group_mean(v):
    r = lax.broadcasted_iota(jnp.int32, (128, 128), 0) // GROUP
    c = lax.broadcasted_iota(jnp.int32, (128, 128), 1) // GROUP
    same = jnp.where(r == c, 1.0 / GROUP, 0.0).astype(jnp.bfloat16)
    high = v.astype(jnp.bfloat16).astype(jnp.float32)
    mid = (v - high).astype(jnp.bfloat16).astype(jnp.float32)
    low = v - high - mid
    y = jnp.dot(
        jnp.concatenate([high, mid, low], axis=0).astype(jnp.bfloat16),
        same,
        preferred_element_type=jnp.float32,
    )
    return y[0:8] + y[8:16] + y[16:24]


def eight(v):
    return jnp.concatenate([v, jnp.zeros((8 - v.shape[0], 128), jnp.float32)], axis=0)


def group_moments(mean, var):
    mean_g = group_mean(mean)
    off = mean - mean_g
    return mean_g, group_mean(var + off * off)


def parts3(v):
    high = v.astype(jnp.bfloat16).astype(jnp.float32)
    mid = (v - high).astype(jnp.bfloat16).astype(jnp.float32)
    return [high, mid, v - high - mid]


def piece_start(core, f):
    low, high = PIECES[3], PIECES[7]
    for i in (2, 1, 0):
        low, high = jnp.where(f == i, PIECES[i], low), jnp.where(f == i, PIECES[4 + i], high)
    return pl.multiple_of(jnp.where(core == 0, low, high), 16)


def k0(tokens_hbm, w_hbm, p0, p1, p2, p3, out_ref, par_ref, tokens_ref, held_ref, in_ref, sems):
    copies = [
        pltpu.make_async_copy(tokens_hbm, tokens_ref, sems.at[0]),
        pltpu.make_async_copy(w_hbm, held_ref.at[:TAPROWS], sems.at[1]),
        pltpu.make_async_copy(p0, in_ref.at[0], sems.at[2]),
        pltpu.make_async_copy(p1, in_ref.at[1], sems.at[3]),
        pltpu.make_async_copy(p2, par_ref.at[0], sems.at[4]),
        pltpu.make_async_copy(p3, par_ref.at[1], sems.at[5]),
    ]
    for copy in copies:
        copy.start()
    for copy in copies:
        copy.wait()
    rows = parts3(in_ref[0]) + parts3(in_ref[1]) + [jnp.zeros((10, 128), jnp.float32)]
    held_ref[TAPROWS:, :] = jnp.concatenate(rows, axis=0).astype(jnp.bfloat16)
    start = piece_start(lax.rem(lax.axis_index("row"), 2), lax.axis_index("frm"))
    piece = jnp.concatenate([held_ref[pl.ds(start, 32), :], held_ref[pl.ds(start + 32, 32), :]], axis=1)
    out_ref[:, :C_LAT, :255] = jnp.broadcast_to(tokens_ref[...][None], (16, C_LAT, 255))
    out_ref[:, C_LAT:, :] = jnp.broadcast_to(piece[None], (16, PIECE // 2, 256))


def k1a(g_ref, up_ref, down_ref, mine_ref):
    for f in range(FRAMES):
        at = slice(16 * f, 16 * f + 16)

        def src(j, lo, hi):
            return g_ref[4 * f + j, :C_LAT, lo:hi]

        up_ref[at, 0:170] = src(0, 0, 170)
        up_ref[at, 176:261] = src(0, 170, 255)
        up_ref[at, 261:346] = src(1, 0, 85)
        down_ref[at, 0:85] = src(2, 170, 255)
        down_ref[at, 85:170] = src(3, 0, 85)
        down_ref[at, 176:346] = src(3, 85, 255)
    for i in range(16):
        mine_ref[i, :32] = g_ref[i, C_LAT:, :128]
        mine_ref[i, 32:] = g_ref[i, C_LAT:, 128:]


def k1(g_ref, above_ref, below_ref, mine_ref, other_ref, pt_ref, wall_ref, st_ref, x_ref):
    core = lax.rem(lax.axis_index("row"), 2)
    for i in range(FRAMES):
        mine, other = piece_start(core, i), piece_start(1 - core, i)
        for j in range(4):
            wall_ref[j, pl.ds(mine, PIECE), :] = mine_ref[4 * i + j]
            wall_ref[j, pl.ds(other, PIECE), :] = other_ref[4 * i + j]
    weight = jnp.concatenate([wall_ref[j, :TAPROWS, :] for j in range(4)], axis=1)
    x_ref[...] = jnp.zeros_like(x_ref)
    pt_ref[: 2 * TAPS, :] = jnp.zeros((2 * TAPS, SPAN), jnp.bfloat16)

    plan = (
        ((0, 0, 170),),
        ((0, 170, 255), (1, 0, 85)),
        ((1, 85, 255),),
        ((2, 0, 170),),
        ((2, 170, 255), (3, 0, 85)),
        ((3, 85, 255),),
    )
    for f in range(FRAMES):
        at = slice(16 * f, 16 * f + 16)
        for row, parts in enumerate(plan):
            lane = LEAD + STRIDE * (row + 2)
            for j, lo, hi in parts:
                x_ref[at, lane : lane + hi - lo] = g_ref[4 * f + j, :C_LAT, lo:hi]
                lane += hi - lo
        for row in range(2):
            lane = LEAD + STRIDE * row
            x_ref[at, lane : lane + W] = above_ref[at, STRIDE * row : STRIDE * row + W]
            lane = LEAD + STRIDE * (row + 8)
            x_ref[at, lane : lane + W] = below_ref[at, STRIDE * row : STRIDE * row + W]
    for f in range(FRAMES):
        for b in range(3):
            for e in range(3):
                at = (f + 2) * TAPS + (3 * b + e) * 16
                lane = LEAD + STRIDE * b + e - 1
                pt_ref[at : at + 16, :] = x_ref[16 * f : 16 * f + 16, lane : lane + SPAN]

    def hidden(g, lo, size):
        return lax.dot_general(
            pt_ref[g * TAPS : (g + 3) * TAPS, lo : lo + size],
            weight,
            (((0,), (0,)), ((), ())),
            preferred_element_type=jnp.float32,
        )

    def valid(lo, size):
        at = lo + lax.broadcasted_iota(jnp.int32, (size, 128), 0)
        ok = (at >= STRIDE) & (at < STRIDE + OWN)
        for row in range(1, 7):
            gap = STRIDE * row + W
            if lo < gap + STRIDE - W and gap < lo + size:
                ok = ok & ((at < gap) | (at >= gap + STRIDE - W))
        return jnp.concatenate([ok] * 4, axis=1)

    pilot = jnp.sum(jnp.where(valid(256, 128), hidden(0, 256, 128), 0.0), axis=0, keepdims=True) * (1.0 / 122)
    s1 = s2 = jnp.zeros((8, CH), jnp.float32)
    for g in range(FRAMES):
        for lo, size in K1_CHUNKS:
            d = jnp.where(valid(lo, size), hidden(g, lo, size) - pilot, 0.0)
            d = d.reshape(size // 8, 8, CH)
            s1 = s1 + jnp.sum(d, axis=0)
            s2 = s2 + jnp.sum(d * d, axis=0)
    n = FRAMES * CELLS
    s1 = jnp.sum(s1, axis=0, keepdims=True)
    s2 = jnp.sum(s2, axis=0, keepdims=True)
    d = s1 / n
    for i, v in enumerate((pilot + d, s2 - s1 * d)):
        for j in range(4):
            part = v[:, 128 * j : 128 * (j + 1)]
            st_ref[:, 4 * i + j : 4 * i + j + 1, :] = jnp.broadcast_to(part[None], (16, 1, 128))


def k2(pt_ref, wall_ref, st_ref, w2_hbm, mix_ref, so_ref, a_ref, w2_ref, y_ref, sem):
    copy = pltpu.make_async_copy(w2_hbm, w2_ref, sem)
    copy.start()
    f, r = lax.axis_index("frm"), lax.axis_index("row")
    weight = jnp.concatenate([wall_ref[j, :TAPROWS, :] for j in range(4)], axis=1)

    def spread3(at):
        rows = [wall_ref[j, TAPROWS:, :].astype(jnp.float32)[at : at + 3] for j in range(4)]
        return jnp.concatenate([jnp.sum(r, axis=0, keepdims=True) for r in rows], axis=1)

    n = FRAMES * CELLS
    st = st_ref[...]
    sums = jnp.sum(st, axis=0)
    means = sums[:4] * (1.0 / 16)
    off = st[:, :4, :] - means[None]
    spread = jnp.sum(off * off, axis=0)
    mean, var = group_moments(eight(means), eight((sums[4:] * (1.0 / n) + spread) * (1.0 / 16)))
    inverse = lax.rsqrt(var + EPSILON)

    def wide(v):
        return jnp.concatenate([v[j : j + 1] for j in range(4)], axis=1)

    mean, scale, shift = wide(mean), 0.5 * wide(inverse) * spread3(0), 0.5 * spread3(3)

    a_ref[0:16, :] = jnp.zeros((16, 3 * CH), jnp.bfloat16)
    a_ref[16 + SPAN :, :] = jnp.zeros((16, 3 * CH), jnp.bfloat16)
    for k in range(3):
        g = f - 2 + k

        @pl.when(g >= 0)
        def _():
            at = pl.multiple_of(g * TAPS, 16)
            for lo, size in CHUNKS:
                h = lax.dot_general(
                    pt_ref[pl.ds(at, 3 * TAPS), lo : lo + size],
                    weight,
                    (((0,), (0,)), ((), ())),
                    preferred_element_type=jnp.float32,
                )
                u = silu_of_twice((h - mean) * scale + shift)
                a_ref[16 + lo : 16 + lo + size, k * CH : (k + 1) * CH] = u.astype(jnp.bfloat16)

        @pl.when(g < 0)
        def _():
            a_ref[16 : 16 + SPAN, k * CH : (k + 1) * CH] = jnp.zeros((SPAN, CH), jnp.bfloat16)

    keep = lax.broadcasted_iota(jnp.int32, (16, 3 * CH), 0) < 10
    for row in range(8):
        at = 16 + STRIDE * row + 160
        a_ref[at : at + 16, :] = jnp.where(keep, a_ref[at : at + 16, :], 0).astype(jnp.bfloat16)

    @pl.when(r == 0)
    def _():
        a_ref[16 : 16 + STRIDE, :] = jnp.zeros((STRIDE, 3 * CH), jnp.bfloat16)

    @pl.when(r == 15)
    def _():
        a_ref[16 + 7 * STRIDE : 16 + SPAN, :] = jnp.zeros((STRIDE, 3 * CH), jnp.bfloat16)

    copy.wait()

    def product(start, rows, *taps):
        kernel = jnp.concatenate(
            [jnp.concatenate([w2_ref[9 * a + 3 * b + e] for a in range(3)], axis=0) for b, e in taps], axis=1
        )
        y_ref[:rows, : 128 * len(taps)] = jnp.dot(
            a_ref[start : start + rows, :], kernel, preferred_element_type=jnp.float32
        )

    for b in range(3):
        product(STRIDE * b, OWN + 32, (b, 0), (b, 2))
        part = y_ref[15 : 15 + OWN, :128] + y_ref[17 : 17 + OWN, 128:]
        mix_ref[...] = part if b == 0 else mix_ref[...] + part
    product(16, SPAN, (0, 1), (2, 1))
    mix_ref[...] += y_ref[0:OWN, :128] + y_ref[2 * STRIDE : 2 * STRIDE + OWN, 128:]
    product(16 + STRIDE, OWN, (1, 1))
    v = (mix_ref[...] + y_ref[0:OWN, :128]).reshape(ROWS, STRIDE, 128)
    mix_ref[...] = v.reshape(OWN, 128)
    ok = lax.broadcasted_iota(jnp.int32, (ROWS, STRIDE, 128), 1) < W
    total = jnp.sum(jnp.sum(jnp.where(ok, v, 0.0), axis=0), axis=0, keepdims=True)
    centre = total / CELLS
    off = jnp.where(ok, v - centre[None], 0.0)
    squares = jnp.sum(jnp.sum(off * off, axis=0), axis=0, keepdims=True)
    so_ref[:, 0:1, :] = jnp.broadcast_to(centre[None], (64, 1, 128))
    so_ref[:, 1:2, :] = jnp.broadcast_to(squares[None], (64, 1, 128))


def k3(mix_ref, st_ref, par_ref, out_ref):
    st = st_ref[...]
    sums = jnp.sum(st, axis=0)
    means = sums * (1.0 / 64)
    off = st - means[None]
    spread = jnp.sum(off * off, axis=0)
    var = (sums[1:2] * (1.0 / CELLS) + spread[0:1]) * (1.0 / 64)
    mean, var = group_moments(eight(means[0:1]), eight(var))
    mean = mean[:1]
    scale = 0.5 * lax.rsqrt(var[:1] + EPSILON) * par_ref[0]
    shift = 0.5 * par_ref[1]
    for row in range(ROWS):
        v = mix_ref[STRIDE * row : STRIDE * (row + 1), :]
        u = silu_of_twice((v - mean) * scale + shift)
        out_ref[0, row] = u[:W].astype(jnp.bfloat16)


def shape(dims, kind):
    return jax.ShapeDtypeStruct(dims, kind)


INHBM = pl.BlockSpec(memory_space=pltpu.HBM)
INVMEM = pl.BlockSpec(memory_space=pltpu.VMEM)


def call_k0(*arrays):
    return pl.pallas_call(
        k0,
        out_shape=(
            shape((16, C_LAT + PIECE // 2, 256), jnp.bfloat16),
            shape((2, 1, 128), jnp.float32),
        ),
        in_specs=[INHBM] * 6,
        out_specs=(INVMEM,) * 2,
        scratch_shapes=[
            pltpu.VMEM((C_LAT, 255), jnp.bfloat16),
            pltpu.VMEM((HELD, 128), jnp.bfloat16),
            pltpu.VMEM((2, 1, 128), jnp.float32),
            pltpu.SemaphoreType.DMA((6,)),
        ],
        compiler_params=pltpu.CompilerParams(vmem_limit_bytes=VMEM),
        name="k0",
    )(*[pltpu.with_memory_space_constraint(v, pltpu.HBM) for v in arrays])


def call_k1a(g):
    return pl.pallas_call(
        k1a,
        out_shape=(
            shape((16 * FRAMES, 2 * STRIDE), jnp.bfloat16),
            shape((16 * FRAMES, 2 * STRIDE), jnp.bfloat16),
            shape((16, PIECE, 128), jnp.bfloat16),
        ),
        in_specs=[INVMEM],
        out_specs=(INVMEM,) * 3,
        compiler_params=pltpu.CompilerParams(vmem_limit_bytes=VMEM),
        name="k1a",
    )(g)


def call_k1(*arrays):
    return pl.pallas_call(
        k1,
        out_shape=(
            shape((6 * TAPS, SPAN), jnp.bfloat16),
            shape((4, HELD, 128), jnp.bfloat16),
            shape((16, 8, 128), jnp.float32),
        ),
        in_specs=[INVMEM] * 5,
        out_specs=(INVMEM,) * 3,
        scratch_shapes=[pltpu.VMEM((16 * FRAMES, XLANES), jnp.bfloat16)],
        compiler_params=pltpu.CompilerParams(vmem_limit_bytes=VMEM),
        name="k1",
    )(*arrays)


def call_k2(pt, wall, st, w2):
    return pl.pallas_call(
        k2,
        out_shape=(shape((OWN, 128), jnp.float32), shape((64, 2, 128), jnp.float32)),
        in_specs=[INVMEM] * 3 + [INHBM],
        out_specs=(INVMEM,) * 2,
        scratch_shapes=[
            pltpu.VMEM((SPAN + 32, 3 * CH), jnp.bfloat16),
            pltpu.VMEM((27, CH, 128), jnp.bfloat16),
            pltpu.VMEM((SPAN, 256), jnp.float32),
            pltpu.SemaphoreType.DMA,
        ],
        compiler_params=pltpu.CompilerParams(vmem_limit_bytes=VMEM),
        name="k2",
    )(pt, wall, st, pltpu.with_memory_space_constraint(w2, pltpu.HBM))


def call_k3(mix, st, par):
    return pl.pallas_call(
        k3,
        out_shape=shape((1, ROWS, W, 128), jnp.bfloat16),
        in_specs=[INVMEM] * 3,
        out_specs=INVMEM,
        compiler_params=pltpu.CompilerParams(vmem_limit_bytes=VMEM),
        name="k3",
    )(mix, st, par)


def per_device(latents, in_weight, in_gain, in_shift, mid_weight, mid_gain, mid_shift):
    params = [v.reshape(1, 128) for v in (in_gain, in_shift, mid_gain, mid_shift)]
    payload, par = call_k0(latents.T, in_weight.reshape(TAPROWS, 128), *params)
    g = lax.all_to_all(payload, ("frm", "ch"), 0, 0)
    up, down, mine = call_k1a(g)
    below = lax.ppermute(up, "row", [(i + 1, i) for i in range(15)])
    above = lax.ppermute(down, "row", [(i, i + 1) for i in range(15)])
    other = lax.ppermute(mine, "row", [(i, i ^ 1) for i in range(16)])
    pt, wall, st = call_k1(g, above, below, mine, other)
    st = lax.all_to_all(st, "row", 0, 0)
    mix, st = call_k2(pt, wall, st, mid_weight)
    st = lax.all_to_all(st, ("frm", "row"), 0, 0)
    return call_k3(mix, st, par)


def solution(mesh):
    return jax.shard_map(
        per_device,
        mesh=mesh,
        in_specs=(
            P(("frm", "row", "ch"), None),
            P(None, None, "ch"),
            P("ch"),
            P("ch"),
            P(None, None, "ch"),
            P("ch"),
            P("ch"),
        ),
        out_specs=P("frm", "row", None, "ch"),
        check_vma=False,
    )
```

```python
import jax
import jax.numpy as jnp
from jax import lax
from jax.experimental import pallas as pl
from jax.experimental.pallas import tpu as pltpu
from jax.sharding import PartitionSpec as P

CH = 512
GROUP = 16
W = 170
ROWS = 6
C_LAT = 16
FRAMES = 4
EPSILON = 1e-06

STRIDE = 176
SPAN = 8 * STRIDE
OWN = ROWS * STRIDE
TAPS = 9 * C_LAT
LEAD = 128
XLANES = 2048
K1_CHUNKS = ((128, 384), (512, 384), (896, 384))
CHUNKS = ((0, 384), (384, 384), (768, 384), (1152, 256))
CELLS = ROWS * W
TAPROWS = 27 * C_LAT
HELD = 448
PIECE = 64
PIECES = tuple(i * 24 // 7 * 16 for i in range(8))
VMEM = 48 * 1024 * 1024


def silu_of_twice(half):
    return half + half * jnp.tanh(half)


def group_mean(v):
    r = lax.broadcasted_iota(jnp.int32, (128, 128), 0) // GROUP
    c = lax.broadcasted_iota(jnp.int32, (128, 128), 1) // GROUP
    same = jnp.where(r == c, 1.0 / GROUP, 0.0).astype(jnp.bfloat16)
    high = v.astype(jnp.bfloat16).astype(jnp.float32)
    mid = (v - high).astype(jnp.bfloat16).astype(jnp.float32)
    low = v - high - mid
    y = jnp.dot(
        jnp.concatenate([high, mid, low], axis=0).astype(jnp.bfloat16),
        same,
        preferred_element_type=jnp.float32,
    )
    return y[0:8] + y[8:16] + y[16:24]


def eight(v):
    return jnp.concatenate([v, jnp.zeros((8 - v.shape[0], 128), jnp.float32)], axis=0)


def group_moments(mean, var):
    mean_g = group_mean(mean)
    off = mean - mean_g
    return mean_g, group_mean(var + off * off)


def parts3(v):
    high = v.astype(jnp.bfloat16).astype(jnp.float32)
    mid = (v - high).astype(jnp.bfloat16).astype(jnp.float32)
    return [high, mid, v - high - mid]


def piece_start(core, f):
    low, high = PIECES[3], PIECES[7]
    for i in (2, 1, 0):
        low, high = jnp.where(f == i, PIECES[i], low), jnp.where(f == i, PIECES[4 + i], high)
    return pl.multiple_of(jnp.where(core == 0, low, high), 16)


def k0(tokens_hbm, w_hbm, p0, p1, p2, p3, out_ref, par_ref, tokens_ref, held_ref, in_ref, sems):
    copies = [
        pltpu.make_async_copy(tokens_hbm, tokens_ref, sems.at[0]),
        pltpu.make_async_copy(w_hbm, held_ref.at[:TAPROWS], sems.at[1]),
        pltpu.make_async_copy(p0, in_ref.at[0], sems.at[2]),
        pltpu.make_async_copy(p1, in_ref.at[1], sems.at[3]),
        pltpu.make_async_copy(p2, par_ref.at[0], sems.at[4]),
        pltpu.make_async_copy(p3, par_ref.at[1], sems.at[5]),
    ]
    for copy in copies:
        copy.start()
    for copy in copies:
        copy.wait()
    rows = parts3(in_ref[0]) + parts3(in_ref[1]) + [jnp.zeros((10, 128), jnp.float32)]
    held_ref[TAPROWS:, :] = jnp.concatenate(rows, axis=0).astype(jnp.bfloat16)
    start = piece_start(lax.rem(lax.axis_index("row"), 2), lax.axis_index("frm"))
    piece = jnp.concatenate([held_ref[pl.ds(start, 32), :], held_ref[pl.ds(start + 32, 32), :]], axis=1)
    out_ref[:, :C_LAT, :255] = jnp.broadcast_to(tokens_ref[...][None], (16, C_LAT, 255))
    out_ref[:, C_LAT:, :] = jnp.broadcast_to(piece[None], (16, PIECE // 2, 256))


def k1a(g_ref, mate_ref, next_ref, first_ref, last_ref):
    first_ref[...] = jnp.zeros_like(first_ref)
    last_ref[...] = jnp.zeros_like(last_ref)
    for f in range(FRAMES):
        at = slice(16 * f, 16 * f + 16)

        def src(j, lo, hi):
            return g_ref[4 * f + j, :C_LAT, lo:hi]

        first_ref[at, 0:170] = src(0, 0, 170)
        first_ref[at, 176:261] = src(0, 170, 255)
        first_ref[at, 261:346] = src(1, 0, 85)
        last_ref[at, 0:85] = src(2, 170, 255)
        last_ref[at, 85:170] = src(3, 0, 85)
        last_ref[at, 176:346] = src(3, 85, 255)
    for i in range(16):
        mate_ref[PIECE * i : PIECE * i + 32] = g_ref[i, C_LAT:, :128]
        mate_ref[PIECE * i + 32 : PIECE * (i + 1)] = g_ref[i, C_LAT:, 128:]

    def send(to_mate, to_next):
        for i in range(3):
            mate_ref[16 * PIECE + 64 * i : 16 * PIECE + 64 * (i + 1)] = to_mate[:, 128 * i : 128 * (i + 1)]
        next_ref[...] = to_next[...]

    core = lax.rem(lax.axis_index("row"), 2)

    @pl.when(core == 0)
    def _():
        send(last_ref, first_ref)

    @pl.when(core == 1)
    def _():
        send(first_ref, last_ref)


def k1(g_ref, mine_ref, other_ref, next_ref, pt_ref, wall_ref, st_ref, x_ref):
    core = lax.rem(lax.axis_index("row"), 2)
    for i in range(FRAMES):
        mine, other = piece_start(core, i), piece_start(1 - core, i)
        for j in range(4):
            wall_ref[j, pl.ds(mine, PIECE), :] = mine_ref[PIECE * (4 * i + j) : PIECE * (4 * i + j + 1)]
            wall_ref[j, pl.ds(other, PIECE), :] = other_ref[PIECE * (4 * i + j) : PIECE * (4 * i + j + 1)]
    weight = jnp.concatenate([wall_ref[j, :TAPROWS, :] for j in range(4)], axis=1)
    x_ref[...] = jnp.zeros_like(x_ref)
    pt_ref[: 2 * TAPS, :] = jnp.zeros((2 * TAPS, SPAN), jnp.bfloat16)

    plan = (
        ((0, 0, 170),),
        ((0, 170, 255), (1, 0, 85)),
        ((1, 85, 255),),
        ((2, 0, 170),),
        ((2, 170, 255), (3, 0, 85)),
        ((3, 85, 255),),
    )
    for f in range(FRAMES):
        at = slice(16 * f, 16 * f + 16)
        for row, parts in enumerate(plan):
            lane = LEAD + STRIDE * (row + 2)
            for j, lo, hi in parts:
                x_ref[at, lane : lane + hi - lo] = g_ref[4 * f + j, :C_LAT, lo:hi]
                lane += hi - lo

    def edges(above, below):
        for f in range(FRAMES):
            at = slice(16 * f, 16 * f + 16)
            for v, row in ((above, 0), (below, 8)):
                lane = LEAD + STRIDE * row
                x_ref[at, lane : lane + 2 * STRIDE] = v(at)

    def from_mate(at):
        parts = [other_ref[16 * PIECE + 64 * i :][at] for i in range(3)]
        return jnp.concatenate(parts, axis=1)[:, : 2 * STRIDE]

    def from_next(at):
        return next_ref[at, : 2 * STRIDE]

    @pl.when(core == 0)
    def _():
        edges(from_next, from_mate)

    @pl.when(core == 1)
    def _():
        edges(from_mate, from_next)

    for f in range(FRAMES):
        for b in range(3):
            for e in range(3):
                at = (f + 2) * TAPS + (3 * b + e) * 16
                lane = LEAD + STRIDE * b + e - 1
                pt_ref[at : at + 16, :] = x_ref[16 * f : 16 * f + 16, lane : lane + SPAN]

    def hidden(g, lo, size):
        return lax.dot_general(
            pt_ref[g * TAPS : (g + 3) * TAPS, lo : lo + size],
            weight,
            (((0,), (0,)), ((), ())),
            preferred_element_type=jnp.float32,
        )

    def valid(lo, size):
        at = lo + lax.broadcasted_iota(jnp.int32, (size, 128), 0)
        ok = (at >= STRIDE) & (at < STRIDE + OWN)
        for row in range(1, 7):
            gap = STRIDE * row + W
            if lo < gap + STRIDE - W and gap < lo + size:
                ok = ok & ((at < gap) | (at >= gap + STRIDE - W))
        return jnp.concatenate([ok] * 4, axis=1)

    pilot = jnp.sum(jnp.where(valid(256, 128), hidden(0, 256, 128), 0.0), axis=0, keepdims=True) * (1.0 / 122)
    s1 = s2 = jnp.zeros((8, CH), jnp.float32)
    for g in range(FRAMES):
        for lo, size in K1_CHUNKS:
            d = jnp.where(valid(lo, size), hidden(g, lo, size) - pilot, 0.0)
            d = d.reshape(size // 8, 8, CH)
            s1 = s1 + jnp.sum(d, axis=0)
            s2 = s2 + jnp.sum(d * d, axis=0)
    n = FRAMES * CELLS
    s1 = jnp.sum(s1, axis=0, keepdims=True)
    s2 = jnp.sum(s2, axis=0, keepdims=True)
    d = s1 / n
    for i, v in enumerate((pilot + d, s2 - s1 * d)):
        for j in range(4):
            part = v[:, 128 * j : 128 * (j + 1)]
            st_ref[:, 4 * i + j : 4 * i + j + 1, :] = jnp.broadcast_to(part[None], (16, 1, 128))


def k2(pt_ref, wall_ref, st_ref, w2_hbm, mix_ref, so_ref, a_ref, w2_ref, y_ref, sem):
    copy = pltpu.make_async_copy(w2_hbm, w2_ref, sem)
    copy.start()
    f, r = lax.axis_index("frm"), lax.axis_index("row")
    weight = jnp.concatenate([wall_ref[j, :TAPROWS, :] for j in range(4)], axis=1)

    def spread3(at):
        rows = [wall_ref[j, TAPROWS:, :].astype(jnp.float32)[at : at + 3] for j in range(4)]
        return jnp.concatenate([jnp.sum(r, axis=0, keepdims=True) for r in rows], axis=1)

    n = FRAMES * CELLS
    st = st_ref[...]
    sums = jnp.sum(st, axis=0)
    means = sums[:4] * (1.0 / 16)
    off = st[:, :4, :] - means[None]
    spread = jnp.sum(off * off, axis=0)
    mean, var = group_moments(eight(means), eight((sums[4:] * (1.0 / n) + spread) * (1.0 / 16)))
    inverse = lax.rsqrt(var + EPSILON)

    def wide(v):
        return jnp.concatenate([v[j : j + 1] for j in range(4)], axis=1)

    mean, scale, shift = wide(mean), 0.5 * wide(inverse) * spread3(0), 0.5 * spread3(3)

    a_ref[0:16, :] = jnp.zeros((16, 3 * CH), jnp.bfloat16)
    a_ref[16 + SPAN :, :] = jnp.zeros((16, 3 * CH), jnp.bfloat16)
    for k in range(3):
        g = f - 2 + k

        @pl.when(g >= 0)
        def _():
            at = pl.multiple_of(g * TAPS, 16)
            for lo, size in CHUNKS:
                h = lax.dot_general(
                    pt_ref[pl.ds(at, 3 * TAPS), lo : lo + size],
                    weight,
                    (((0,), (0,)), ((), ())),
                    preferred_element_type=jnp.float32,
                )
                u = silu_of_twice((h - mean) * scale + shift)
                a_ref[16 + lo : 16 + lo + size, k * CH : (k + 1) * CH] = u.astype(jnp.bfloat16)

        @pl.when(g < 0)
        def _():
            a_ref[16 : 16 + SPAN, k * CH : (k + 1) * CH] = jnp.zeros((SPAN, CH), jnp.bfloat16)

    keep = lax.broadcasted_iota(jnp.int32, (16, 3 * CH), 0) < 10
    for row in range(8):
        at = 16 + STRIDE * row + 160
        a_ref[at : at + 16, :] = jnp.where(keep, a_ref[at : at + 16, :], 0).astype(jnp.bfloat16)

    @pl.when(r == 0)
    def _():
        a_ref[16 : 16 + STRIDE, :] = jnp.zeros((STRIDE, 3 * CH), jnp.bfloat16)

    @pl.when(r == 15)
    def _():
        a_ref[16 + 7 * STRIDE : 16 + SPAN, :] = jnp.zeros((STRIDE, 3 * CH), jnp.bfloat16)

    copy.wait()

    def product(start, rows, *taps):
        kernel = jnp.concatenate(
            [jnp.concatenate([w2_ref[9 * a + 3 * b + e] for a in range(3)], axis=0) for b, e in taps], axis=1
        )
        y_ref[:rows, : 128 * len(taps)] = jnp.dot(
            a_ref[start : start + rows, :], kernel, preferred_element_type=jnp.float32
        )

    for b in range(3):
        product(STRIDE * b, OWN + 32, (b, 0), (b, 2))
        part = y_ref[15 : 15 + OWN, :128] + y_ref[17 : 17 + OWN, 128:]
        mix_ref[...] = part if b == 0 else mix_ref[...] + part
    product(16, SPAN, (0, 1), (2, 1))
    mix_ref[...] += y_ref[0:OWN, :128] + y_ref[2 * STRIDE : 2 * STRIDE + OWN, 128:]
    product(16 + STRIDE, OWN, (1, 1))
    v = (mix_ref[...] + y_ref[0:OWN, :128]).reshape(ROWS, STRIDE, 128)
    mix_ref[...] = v.reshape(OWN, 128)
    ok = lax.broadcasted_iota(jnp.int32, (ROWS, STRIDE, 128), 1) < W
    total = jnp.sum(jnp.sum(jnp.where(ok, v, 0.0), axis=0), axis=0, keepdims=True)
    centre = total / CELLS
    off = jnp.where(ok, v - centre[None], 0.0)
    squares = jnp.sum(jnp.sum(off * off, axis=0), axis=0, keepdims=True)
    so_ref[:, 0:1, :] = jnp.broadcast_to(centre[None], (64, 1, 128))
    so_ref[:, 1:2, :] = jnp.broadcast_to(squares[None], (64, 1, 128))


def k3(mix_ref, st_ref, par_ref, out_ref):
    st = st_ref[...]
    sums = jnp.sum(st, axis=0)
    means = sums * (1.0 / 64)
    off = st - means[None]
    spread = jnp.sum(off * off, axis=0)
    var = (sums[1:2] * (1.0 / CELLS) + spread[0:1]) * (1.0 / 64)
    mean, var = group_moments(eight(means[0:1]), eight(var))
    mean = mean[:1]
    scale = 0.5 * lax.rsqrt(var[:1] + EPSILON) * par_ref[0]
    shift = 0.5 * par_ref[1]
    for row in range(ROWS):
        v = mix_ref[STRIDE * row : STRIDE * (row + 1), :]
        u = silu_of_twice((v - mean) * scale + shift)
        out_ref[0, row] = u[:W].astype(jnp.bfloat16)


def shape(dims, kind):
    return jax.ShapeDtypeStruct(dims, kind)


INHBM = pl.BlockSpec(memory_space=pltpu.HBM)
INVMEM = pl.BlockSpec(memory_space=pltpu.VMEM)


def call_k0(*arrays):
    return pl.pallas_call(
        k0,
        out_shape=(
            shape((16, C_LAT + PIECE // 2, 256), jnp.bfloat16),
            shape((2, 1, 128), jnp.float32),
        ),
        in_specs=[INHBM] * 6,
        out_specs=(INVMEM,) * 2,
        scratch_shapes=[
            pltpu.VMEM((C_LAT, 255), jnp.bfloat16),
            pltpu.VMEM((HELD, 128), jnp.bfloat16),
            pltpu.VMEM((2, 1, 128), jnp.float32),
            pltpu.SemaphoreType.DMA((6,)),
        ],
        compiler_params=pltpu.CompilerParams(vmem_limit_bytes=VMEM),
        name="k0",
    )(*[pltpu.with_memory_space_constraint(v, pltpu.HBM) for v in arrays])


def call_k1a(g):
    edge = (16 * FRAMES, 384)
    return pl.pallas_call(
        k1a,
        out_shape=(
            shape((16 * PIECE + 3 * 64, 128), jnp.bfloat16),
            shape(edge, jnp.bfloat16),
        ),
        in_specs=[INVMEM],
        out_specs=(INVMEM,) * 2,
        scratch_shapes=[pltpu.VMEM(edge, jnp.bfloat16)] * 2,
        compiler_params=pltpu.CompilerParams(vmem_limit_bytes=VMEM),
        name="k1a",
    )(g)


def call_k1(*arrays):
    return pl.pallas_call(
        k1,
        out_shape=(
            shape((6 * TAPS, SPAN), jnp.bfloat16),
            shape((4, HELD, 128), jnp.bfloat16),
            shape((16, 8, 128), jnp.float32),
        ),
        in_specs=[INVMEM] * 4,
        out_specs=(INVMEM,) * 3,
        scratch_shapes=[pltpu.VMEM((16 * FRAMES, XLANES), jnp.bfloat16)],
        compiler_params=pltpu.CompilerParams(vmem_limit_bytes=VMEM),
        name="k1",
    )(*arrays)


def call_k2(pt, wall, st, w2):
    return pl.pallas_call(
        k2,
        out_shape=(shape((OWN, 128), jnp.float32), shape((64, 2, 128), jnp.float32)),
        in_specs=[INVMEM] * 3 + [INHBM],
        out_specs=(INVMEM,) * 2,
        scratch_shapes=[
            pltpu.VMEM((SPAN + 32, 3 * CH), jnp.bfloat16),
            pltpu.VMEM((27, CH, 128), jnp.bfloat16),
            pltpu.VMEM((SPAN, 256), jnp.float32),
            pltpu.SemaphoreType.DMA,
        ],
        compiler_params=pltpu.CompilerParams(vmem_limit_bytes=VMEM),
        name="k2",
    )(pt, wall, st, pltpu.with_memory_space_constraint(w2, pltpu.HBM))


def call_k3(mix, st, par):
    return pl.pallas_call(
        k3,
        out_shape=shape((1, ROWS, W, 128), jnp.bfloat16),
        in_specs=[INVMEM] * 3,
        out_specs=INVMEM,
        compiler_params=pltpu.CompilerParams(vmem_limit_bytes=VMEM),
        name="k3",
    )(mix, st, par)


def per_device(latents, in_weight, in_gain, in_shift, mid_weight, mid_gain, mid_shift):
    params = [v.reshape(1, 128) for v in (in_gain, in_shift, mid_gain, mid_shift)]
    payload, par = call_k0(latents.T, in_weight.reshape(TAPROWS, 128), *params)
    g = lax.all_to_all(payload, ("frm", "ch"), 0, 0)
    mine, edge = call_k1a(g)
    other = lax.ppermute(mine, "row", [(i, i ^ 1) for i in range(16)])
    edge = lax.ppermute(edge, "row", [(i, i + 2 * (i % 2) - 1) for i in range(1, 15)])
    pt, wall, st = call_k1(g, mine, other, edge)
    st = lax.all_to_all(st, "row", 0, 0)
    mix, st = call_k2(pt, wall, st, mid_weight)
    st = lax.all_to_all(st, ("frm", "row"), 0, 0)
    return call_k3(mix, st, par)


def solution(mesh):
    return jax.shard_map(
        per_device,
        mesh=mesh,
        in_specs=(
            P(("frm", "row", "ch"), None),
            P(None, None, "ch"),
            P("ch"),
            P("ch"),
            P(None, None, "ch"),
            P("ch"),
            P("ch"),
        ),
        out_specs=P("frm", "row", None, "ch"),
        check_vma=False,
    )
```

```python
import jax
import jax.numpy as jnp
from jax import lax
from jax.experimental import pallas as pl
from jax.experimental.pallas import tpu as pltpu
from jax.sharding import PartitionSpec as P

CH = 512
GROUP = 16
W = 170
ROWS = 6
C_LAT = 16
FRAMES = 4
EPSILON = 1e-06

STRIDE = 176
SPAN = 8 * STRIDE
OWN = ROWS * STRIDE
TAPS = 9 * C_LAT
LEAD = 128
XLANES = 2048
K1_CHUNKS = ((128, 384), (512, 384), (896, 384))
CHUNKS = ((0, 384), (384, 384), (768, 384), (1152, 256))
CELLS = ROWS * W
TAPROWS = 27 * C_LAT
HELD = 448
HALF = HELD // 2
EDGE = HELD + HALF
VMEM = 48 * 1024 * 1024


def silu_of_twice(half):
    return half + half * jnp.tanh(half)


def group_mean(v):
    r = lax.broadcasted_iota(jnp.int32, (128, 128), 0) // GROUP
    c = lax.broadcasted_iota(jnp.int32, (128, 128), 1) // GROUP
    same = jnp.where(r == c, 1.0 / GROUP, 0.0).astype(jnp.bfloat16)
    high = v.astype(jnp.bfloat16).astype(jnp.float32)
    mid = (v - high).astype(jnp.bfloat16).astype(jnp.float32)
    low = v - high - mid
    y = jnp.dot(
        jnp.concatenate([high, mid, low], axis=0).astype(jnp.bfloat16),
        same,
        preferred_element_type=jnp.float32,
    )
    return y[0:8] + y[8:16] + y[16:24]


def eight(v):
    return jnp.concatenate([v, jnp.zeros((8 - v.shape[0], 128), jnp.float32)], axis=0)


def group_moments(mean, var):
    mean_g = group_mean(mean)
    off = mean - mean_g
    return mean_g, group_mean(var + off * off)


def parts3(v):
    high = v.astype(jnp.bfloat16).astype(jnp.float32)
    mid = (v - high).astype(jnp.bfloat16).astype(jnp.float32)
    return [high, mid, v - high - mid]


def k0(tokens_hbm, w_hbm, p0, p1, p2, p3, out_ref, held_ref, half_ref, par_ref, tokens_ref, in_ref, sems):
    copies = [
        pltpu.make_async_copy(tokens_hbm, tokens_ref, sems.at[0]),
        pltpu.make_async_copy(w_hbm, held_ref.at[:TAPROWS], sems.at[1]),
        pltpu.make_async_copy(p0, in_ref.at[0], sems.at[2]),
        pltpu.make_async_copy(p1, in_ref.at[1], sems.at[3]),
        pltpu.make_async_copy(p2, par_ref.at[0], sems.at[4]),
        pltpu.make_async_copy(p3, par_ref.at[1], sems.at[5]),
    ]
    for copy in copies:
        copy.start()
    for copy in copies:
        copy.wait()
    rows = parts3(in_ref[0]) + parts3(in_ref[1]) + [jnp.zeros((10, 128), jnp.float32)]
    held_ref[TAPROWS:, :] = jnp.concatenate(rows, axis=0).astype(jnp.bfloat16)
    start = pl.multiple_of(lax.rem(lax.axis_index("row"), 2) * HALF, 16)
    half_ref[...] = held_ref[pl.ds(start, HALF), :]
    out_ref[...] = jnp.broadcast_to(tokens_ref[...][None], (16, C_LAT, 255))


def first_rows(g_ref, f):
    return ((0, g_ref[4 * f, :, :170]), (176, g_ref[4 * f, :, 170:255]), (261, g_ref[4 * f + 1, :, :85]))


def last_rows(g_ref, f):
    return ((0, g_ref[4 * f + 2, :, 170:255]), (85, g_ref[4 * f + 3, :, :85]), (176, g_ref[4 * f + 3, :, 85:255]))


def write_edge(rows, g_ref, out_ref):
    for f in range(FRAMES):
        for lane, v in rows(g_ref, f):
            out_ref[16 * f : 16 * f + 16, lane : lane + v.shape[1]] = v


def k1t(g_ref, next_ref):
    next_ref[...] = jnp.zeros_like(next_ref)
    core = lax.rem(lax.axis_index("row"), 2)

    @pl.when(core == 0)
    def _():
        write_edge(first_rows, g_ref, next_ref)

    @pl.when(core == 1)
    def _():
        write_edge(last_rows, g_ref, next_ref)


def k1w(g_ref, side_ref, far_ref, next_ref, mate_ref, x_ref, edge_ref):
    mate_ref[:HELD] = side_ref[...]
    mate_ref[HELD:EDGE] = far_ref[...]
    edge_ref[...] = jnp.zeros_like(edge_ref)
    x_ref[...] = jnp.zeros_like(x_ref)
    core = lax.rem(lax.axis_index("row"), 2)

    @pl.when(core == 0)
    def _():
        write_edge(last_rows, g_ref, edge_ref)
        x_ref[:, LEAD : LEAD + 2 * STRIDE] = next_ref[:, : 2 * STRIDE]

    @pl.when(core == 1)
    def _():
        write_edge(first_rows, g_ref, edge_ref)
        x_ref[:, LEAD + 8 * STRIDE : LEAD + 10 * STRIDE] = next_ref[:, : 2 * STRIDE]

    for i in range(3):
        mate_ref[EDGE + 64 * i : EDGE + 64 * (i + 1)] = edge_ref[:, 128 * i : 128 * (i + 1)]
    plan = (
        ((0, 0, 170),),
        ((0, 170, 255), (1, 0, 85)),
        ((1, 85, 255),),
        ((2, 0, 170),),
        ((2, 170, 255), (3, 0, 85)),
        ((3, 85, 255),),
    )
    for f in range(FRAMES):
        at = slice(16 * f, 16 * f + 16)
        for row, parts in enumerate(plan):
            lane = LEAD + STRIDE * (row + 2)
            for j, lo, hi in parts:
                x_ref[at, lane : lane + hi - lo] = g_ref[4 * f + j, :, lo:hi]
                lane += hi - lo


def k1(x_in_ref, held_ref, mine_ref, other_ref, pt_ref, wall_ref, st_ref, x_ref):
    c, core = lax.axis_index("ch"), lax.rem(lax.axis_index("row"), 2)
    wall_ref[c] = held_ref[...]
    wall_ref[lax.rem(c + 1 + 2 * core, 4)] = mine_ref[:HELD, :]
    wall_ref[lax.rem(c + 3 - 2 * core, 4)] = other_ref[:HELD, :]
    far = lax.rem(c + 2, 4)
    wall_ref[far, pl.ds(pl.multiple_of(core * HALF, 16), HALF), :] = mine_ref[HELD:EDGE, :]
    wall_ref[far, pl.ds(pl.multiple_of((1 - core) * HALF, 16), HALF), :] = other_ref[HELD:EDGE, :]
    weight = jnp.concatenate([wall_ref[j, :TAPROWS, :] for j in range(4)], axis=1)
    x_ref[...] = x_in_ref[...]
    pt_ref[: 2 * TAPS, :] = jnp.zeros((2 * TAPS, SPAN), jnp.bfloat16)
    parts = [other_ref[EDGE + 64 * i : EDGE + 64 * (i + 1)] for i in range(3)]
    edge = jnp.concatenate(parts, axis=1)[:, : 2 * STRIDE]

    @pl.when(core == 0)
    def _():
        x_ref[:, LEAD + 8 * STRIDE : LEAD + 10 * STRIDE] = edge

    @pl.when(core == 1)
    def _():
        x_ref[:, LEAD : LEAD + 2 * STRIDE] = edge

    for f in range(FRAMES):
        for b in range(3):
            for e in range(3):
                at = (f + 2) * TAPS + (3 * b + e) * 16
                lane = LEAD + STRIDE * b + e - 1
                pt_ref[at : at + 16, :] = x_ref[16 * f : 16 * f + 16, lane : lane + SPAN]

    def hidden(g, lo, size):
        return lax.dot_general(
            pt_ref[g * TAPS : (g + 3) * TAPS, lo : lo + size],
            weight,
            (((0,), (0,)), ((), ())),
            preferred_element_type=jnp.float32,
        )

    def valid(lo, size):
        at = lo + lax.broadcasted_iota(jnp.int32, (size, 128), 0)
        ok = (at >= STRIDE) & (at < STRIDE + OWN)
        for row in range(1, 7):
            gap = STRIDE * row + W
            if lo < gap + STRIDE - W and gap < lo + size:
                ok = ok & ((at < gap) | (at >= gap + STRIDE - W))
        return jnp.concatenate([ok] * 4, axis=1)

    pilot = jnp.sum(jnp.where(valid(256, 128), hidden(0, 256, 128), 0.0), axis=0, keepdims=True) * (1.0 / 122)
    s1 = s2 = jnp.zeros((8, CH), jnp.float32)
    for g in range(FRAMES):
        for lo, size in K1_CHUNKS:
            d = jnp.where(valid(lo, size), hidden(g, lo, size) - pilot, 0.0)
            d = d.reshape(size // 8, 8, CH)
            s1 = s1 + jnp.sum(d, axis=0)
            s2 = s2 + jnp.sum(d * d, axis=0)
    n = FRAMES * CELLS
    s1 = jnp.sum(s1, axis=0, keepdims=True)
    s2 = jnp.sum(s2, axis=0, keepdims=True)
    d = s1 / n
    for i, v in enumerate((pilot + d, s2 - s1 * d)):
        for j in range(4):
            part = v[:, 128 * j : 128 * (j + 1)]
            st_ref[:, 4 * i + j : 4 * i + j + 1, :] = jnp.broadcast_to(part[None], (16, 1, 128))


def k2(pt_ref, wall_ref, st_ref, w2_hbm, mix_ref, so_ref, a_ref, w2_ref, y_ref, sem):
    copy = pltpu.make_async_copy(w2_hbm, w2_ref, sem)
    copy.start()
    f, r = lax.axis_index("frm"), lax.axis_index("row")
    weight = jnp.concatenate([wall_ref[j, :TAPROWS, :] for j in range(4)], axis=1)

    def spread3(at):
        rows = [wall_ref[j, TAPROWS:, :].astype(jnp.float32)[at : at + 3] for j in range(4)]
        return jnp.concatenate([jnp.sum(r, axis=0, keepdims=True) for r in rows], axis=1)

    n = FRAMES * CELLS
    st = st_ref[...]
    sums = jnp.sum(st, axis=0)
    means = sums[:4] * (1.0 / 16)
    off = st[:, :4, :] - means[None]
    spread = jnp.sum(off * off, axis=0)
    mean, var = group_moments(eight(means), eight((sums[4:] * (1.0 / n) + spread) * (1.0 / 16)))
    inverse = lax.rsqrt(var + EPSILON)

    def wide(v):
        return jnp.concatenate([v[j : j + 1] for j in range(4)], axis=1)

    mean, scale, shift = wide(mean), 0.5 * wide(inverse) * spread3(0), 0.5 * spread3(3)

    a_ref[0:16, :] = jnp.zeros((16, 3 * CH), jnp.bfloat16)
    a_ref[16 + SPAN :, :] = jnp.zeros((16, 3 * CH), jnp.bfloat16)
    for k in range(3):
        g = f - 2 + k

        @pl.when(g >= 0)
        def _():
            at = pl.multiple_of(g * TAPS, 16)
            for lo, size in CHUNKS:
                h = lax.dot_general(
                    pt_ref[pl.ds(at, 3 * TAPS), lo : lo + size],
                    weight,
                    (((0,), (0,)), ((), ())),
                    preferred_element_type=jnp.float32,
                )
                u = silu_of_twice((h - mean) * scale + shift)
                a_ref[16 + lo : 16 + lo + size, k * CH : (k + 1) * CH] = u.astype(jnp.bfloat16)

        @pl.when(g < 0)
        def _():
            a_ref[16 : 16 + SPAN, k * CH : (k + 1) * CH] = jnp.zeros((SPAN, CH), jnp.bfloat16)

    keep = lax.broadcasted_iota(jnp.int32, (16, 3 * CH), 0) < 10
    for row in range(8):
        at = 16 + STRIDE * row + 160
        a_ref[at : at + 16, :] = jnp.where(keep, a_ref[at : at + 16, :], 0).astype(jnp.bfloat16)

    @pl.when(r == 0)
    def _():
        a_ref[16 : 16 + STRIDE, :] = jnp.zeros((STRIDE, 3 * CH), jnp.bfloat16)

    @pl.when(r == 15)
    def _():
        a_ref[16 + 7 * STRIDE : 16 + SPAN, :] = jnp.zeros((STRIDE, 3 * CH), jnp.bfloat16)

    copy.wait()

    def product(start, rows, *taps):
        kernel = jnp.concatenate(
            [jnp.concatenate([w2_ref[9 * a + 3 * b + e] for a in range(3)], axis=0) for b, e in taps], axis=1
        )
        y_ref[:rows, : 128 * len(taps)] = jnp.dot(
            a_ref[start : start + rows, :], kernel, preferred_element_type=jnp.float32
        )

    for b in range(3):
        product(STRIDE * b, OWN + 32, (b, 0), (b, 2))
        part = y_ref[15 : 15 + OWN, :128] + y_ref[17 : 17 + OWN, 128:]
        mix_ref[...] = part if b == 0 else mix_ref[...] + part
    product(16, SPAN, (0, 1), (2, 1))
    mix_ref[...] += y_ref[0:OWN, :128] + y_ref[2 * STRIDE : 2 * STRIDE + OWN, 128:]
    product(16 + STRIDE, OWN, (1, 1))
    v = (mix_ref[...] + y_ref[0:OWN, :128]).reshape(ROWS, STRIDE, 128)
    mix_ref[...] = v.reshape(OWN, 128)
    ok = lax.broadcasted_iota(jnp.int32, (ROWS, STRIDE, 128), 1) < W
    total = jnp.sum(jnp.sum(jnp.where(ok, v, 0.0), axis=0), axis=0, keepdims=True)
    centre = total / CELLS
    off = jnp.where(ok, v - centre[None], 0.0)
    squares = jnp.sum(jnp.sum(off * off, axis=0), axis=0, keepdims=True)
    so_ref[:, 0:1, :] = jnp.broadcast_to(centre[None], (64, 1, 128))
    so_ref[:, 1:2, :] = jnp.broadcast_to(squares[None], (64, 1, 128))


def k3(mix_ref, st_ref, par_ref, out_ref):
    st = st_ref[...]
    sums = jnp.sum(st, axis=0)
    means = sums * (1.0 / 64)
    off = st - means[None]
    spread = jnp.sum(off * off, axis=0)
    var = (sums[1:2] * (1.0 / CELLS) + spread[0:1]) * (1.0 / 64)
    mean, var = group_moments(eight(means[0:1]), eight(var))
    mean = mean[:1]
    scale = 0.5 * lax.rsqrt(var[:1] + EPSILON) * par_ref[0]
    shift = 0.5 * par_ref[1]
    for row in range(ROWS):
        v = mix_ref[STRIDE * row : STRIDE * (row + 1), :]
        u = silu_of_twice((v - mean) * scale + shift)
        out_ref[0, row] = u[:W].astype(jnp.bfloat16)


def shape(dims, kind):
    return jax.ShapeDtypeStruct(dims, kind)


INHBM = pl.BlockSpec(memory_space=pltpu.HBM)
INVMEM = pl.BlockSpec(memory_space=pltpu.VMEM)


def call_k0(*arrays):
    return pl.pallas_call(
        k0,
        out_shape=(
            shape((16, C_LAT, 255), jnp.bfloat16),
            shape((HELD, 128), jnp.bfloat16),
            shape((HALF, 128), jnp.bfloat16),
            shape((2, 1, 128), jnp.float32),
        ),
        in_specs=[INHBM] * 6,
        out_specs=(INVMEM,) * 4,
        scratch_shapes=[
            pltpu.VMEM((C_LAT, 255), jnp.bfloat16),
            pltpu.VMEM((2, 1, 128), jnp.float32),
            pltpu.SemaphoreType.DMA((6,)),
        ],
        compiler_params=pltpu.CompilerParams(vmem_limit_bytes=VMEM),
        name="k0",
    )(*[pltpu.with_memory_space_constraint(v, pltpu.HBM) for v in arrays])


def call_k1t(g):
    return pl.pallas_call(
        k1t,
        out_shape=shape((16 * FRAMES, 384), jnp.bfloat16),
        in_specs=[INVMEM],
        out_specs=INVMEM,
        compiler_params=pltpu.CompilerParams(vmem_limit_bytes=VMEM),
        name="k1t",
    )(g)


def call_k1w(*arrays):
    return pl.pallas_call(
        k1w,
        out_shape=(
            shape((EDGE + 3 * 64, 128), jnp.bfloat16),
            shape((16 * FRAMES, XLANES), jnp.bfloat16),
        ),
        in_specs=[INVMEM] * 4,
        out_specs=(INVMEM,) * 2,
        scratch_shapes=[pltpu.VMEM((16 * FRAMES, 384), jnp.bfloat16)],
        compiler_params=pltpu.CompilerParams(vmem_limit_bytes=VMEM),
        name="k1w",
    )(*arrays)


def call_k1(*arrays):
    return pl.pallas_call(
        k1,
        out_shape=(
            shape((6 * TAPS, SPAN), jnp.bfloat16),
            shape((4, HELD, 128), jnp.bfloat16),
            shape((16, 8, 128), jnp.float32),
        ),
        in_specs=[INVMEM] * 4,
        out_specs=(INVMEM,) * 3,
        scratch_shapes=[pltpu.VMEM((16 * FRAMES, XLANES), jnp.bfloat16)],
        compiler_params=pltpu.CompilerParams(vmem_limit_bytes=VMEM),
        name="k1",
    )(*arrays)


def call_k2(pt, wall, st, w2):
    return pl.pallas_call(
        k2,
        out_shape=(shape((OWN, 128), jnp.float32), shape((64, 2, 128), jnp.float32)),
        in_specs=[INVMEM] * 3 + [INHBM],
        out_specs=(INVMEM,) * 2,
        scratch_shapes=[
            pltpu.VMEM((SPAN + 32, 3 * CH), jnp.bfloat16),
            pltpu.VMEM((27, CH, 128), jnp.bfloat16),
            pltpu.VMEM((SPAN, 256), jnp.float32),
            pltpu.SemaphoreType.DMA,
        ],
        compiler_params=pltpu.CompilerParams(vmem_limit_bytes=VMEM),
        name="k2",
    )(pt, wall, st, pltpu.with_memory_space_constraint(w2, pltpu.HBM))


def call_k3(mix, st, par):
    return pl.pallas_call(
        k3,
        out_shape=shape((1, ROWS, W, 128), jnp.bfloat16),
        in_specs=[INVMEM] * 3,
        out_specs=INVMEM,
        compiler_params=pltpu.CompilerParams(vmem_limit_bytes=VMEM),
        name="k3",
    )(mix, st, par)


def per_device(latents, in_weight, in_gain, in_shift, mid_weight, mid_gain, mid_shift):
    params = [v.reshape(1, 128) for v in (in_gain, in_shift, mid_gain, mid_shift)]
    payload, held, half, par = call_k0(latents.T, in_weight.reshape(TAPROWS, 128), *params)
    g = lax.all_to_all(payload, ("frm", "ch"), 0, 0)
    sides = [(4 * i + (j + 1 + 2 * (i % 2)) % 4, 4 * i + j) for i in range(16) for j in range(4)]
    side = lax.ppermute(held, ("row", "ch"), sides)
    fars = [(4 * (i ^ 8) + (j + 2) % 4, 4 * i + j) for i in range(16) for j in range(4)]
    far = lax.ppermute(half, ("row", "ch"), fars)
    edge = lax.ppermute(call_k1t(g), "row", [(i, i + 2 * (i % 2) - 1) for i in range(1, 15)])
    mine, x = call_k1w(g, side, far, edge)
    other = lax.ppermute(mine, "row", [(i, i ^ 1) for i in range(16)])
    pt, wall, st = call_k1(x, held, mine, other)
    st = lax.all_to_all(st, "row", 0, 0)
    mix, st = call_k2(pt, wall, st, mid_weight)
    st = lax.all_to_all(st, ("frm", "row"), 0, 0)
    return call_k3(mix, st, par)


def solution(mesh):
    return jax.shard_map(
        per_device,
        mesh=mesh,
        in_specs=(
            P(("frm", "row", "ch"), None),
            P(None, None, "ch"),
            P("ch"),
            P("ch"),
            P(None, None, "ch"),
            P("ch"),
            P("ch"),
        ),
        out_specs=P("frm", "row", None, "ch"),
        check_vma=False,
    )
```

```python
import jax
import jax.numpy as jnp
from jax import lax
from jax.experimental import pallas as pl
from jax.experimental.pallas import tpu as pltpu
from jax.sharding import PartitionSpec as P

CH = 512
GROUP = 16
W = 170
ROWS = 6
C_LAT = 16
FRAMES = 4
EPSILON = 1e-06

STRIDE = 176
SPAN = 8 * STRIDE
OWN = ROWS * STRIDE
TAPS = 9 * C_LAT
LEAD = 128
XLANES = 2048
K1_CHUNKS = ((128, 640), (768, 512))
CHUNKS = ((0, 384), (384, 384), (768, 384), (1152, 256))
CELLS = ROWS * W
TAPROWS = 27 * C_LAT
HELD = 448
HALF = HELD // 2
VMEM = 48 * 1024 * 1024


def silu_of_twice(half):
    return half + half * jnp.tanh(half)


def group_mean(v):
    r = lax.broadcasted_iota(jnp.int32, (128, 128), 0) // GROUP
    c = lax.broadcasted_iota(jnp.int32, (128, 128), 1) // GROUP
    same = jnp.where(r == c, 1.0 / GROUP, 0.0).astype(jnp.bfloat16)
    high = v.astype(jnp.bfloat16).astype(jnp.float32)
    mid = (v - high).astype(jnp.bfloat16).astype(jnp.float32)
    low = v - high - mid
    y = jnp.dot(
        jnp.concatenate([high, mid, low], axis=0).astype(jnp.bfloat16),
        same,
        preferred_element_type=jnp.float32,
    )
    return y[0:8] + y[8:16] + y[16:24]


def eight(v):
    return jnp.concatenate([v, jnp.zeros((8 - v.shape[0], 128), jnp.float32)], axis=0)


def group_moments(mean, var):
    mean_g = group_mean(mean)
    off = mean - mean_g
    return mean_g, group_mean(var + off * off)


def parts3(v):
    high = v.astype(jnp.bfloat16).astype(jnp.float32)
    mid = (v - high).astype(jnp.bfloat16).astype(jnp.float32)
    return [high, mid, v - high - mid]


def k0(tokens_hbm, w_hbm, p0, p1, p2, p3, out_ref, held_ref, half_ref, par_ref, tokens_ref, in_ref, sems):
    copies = [
        pltpu.make_async_copy(tokens_hbm, tokens_ref, sems.at[0]),
        pltpu.make_async_copy(w_hbm, held_ref.at[:TAPROWS], sems.at[1]),
        pltpu.make_async_copy(p0, in_ref.at[0], sems.at[2]),
        pltpu.make_async_copy(p1, in_ref.at[1], sems.at[3]),
        pltpu.make_async_copy(p2, par_ref.at[0], sems.at[4]),
        pltpu.make_async_copy(p3, par_ref.at[1], sems.at[5]),
    ]
    for copy in copies:
        copy.start()
    for copy in copies:
        copy.wait()
    rows = parts3(in_ref[0]) + parts3(in_ref[1]) + [jnp.zeros((10, 128), jnp.float32)]
    held_ref[TAPROWS:, :] = jnp.concatenate(rows, axis=0).astype(jnp.bfloat16)
    start = pl.multiple_of(lax.rem(lax.axis_index("row"), 2) * HALF, 16)
    half_ref[...] = held_ref[pl.ds(start, HALF), :]
    out_ref[...] = jnp.broadcast_to(tokens_ref[...][None], (16, C_LAT, 255))


def first_rows(g_ref, f):
    return ((0, g_ref[4 * f, :, :170]), (176, g_ref[4 * f, :, 170:255]), (261, g_ref[4 * f + 1, :, :85]))


def last_rows(g_ref, f):
    return ((0, g_ref[4 * f + 2, :, 170:255]), (85, g_ref[4 * f + 3, :, :85]), (176, g_ref[4 * f + 3, :, 85:255]))


def write_edge(rows, g_ref, out_ref):
    for f in range(FRAMES):
        for lane, v in rows(g_ref, f):
            out_ref[16 * f : 16 * f + 16, lane : lane + v.shape[1]] = v


def k1t(g_ref, next_ref, mate_ref):
    next_ref[...] = jnp.zeros_like(next_ref)
    mate_ref[...] = jnp.zeros_like(mate_ref)
    core = lax.rem(lax.axis_index("row"), 2)

    @pl.when(core == 0)
    def _():
        write_edge(first_rows, g_ref, next_ref)
        write_edge(last_rows, g_ref, mate_ref)

    @pl.when(core == 1)
    def _():
        write_edge(last_rows, g_ref, next_ref)
        write_edge(first_rows, g_ref, mate_ref)


def k1w(g_ref, side_ref, far_ref, next_ref, mate_ref, both_ref, x_ref):
    both_ref[:HELD] = side_ref[...]
    both_ref[HELD:] = far_ref[...]
    x_ref[...] = jnp.zeros_like(x_ref)
    core = lax.rem(lax.axis_index("row"), 2)

    def edges(above_ref, below_ref):
        x_ref[:, LEAD : LEAD + 2 * STRIDE] = above_ref[:, : 2 * STRIDE]
        x_ref[:, LEAD + 8 * STRIDE : LEAD + 10 * STRIDE] = below_ref[:, : 2 * STRIDE]

    @pl.when(core == 0)
    def _():
        edges(next_ref, mate_ref)

    @pl.when(core == 1)
    def _():
        edges(mate_ref, next_ref)

    plan = (
        ((0, 0, 170),),
        ((0, 170, 255), (1, 0, 85)),
        ((1, 85, 255),),
        ((2, 0, 170),),
        ((2, 170, 255), (3, 0, 85)),
        ((3, 85, 255),),
    )
    for f in range(FRAMES):
        at = slice(16 * f, 16 * f + 16)
        for row, parts in enumerate(plan):
            lane = LEAD + STRIDE * (row + 2)
            for j, lo, hi in parts:
                x_ref[at, lane : lane + hi - lo] = g_ref[4 * f + j, :, lo:hi]
                lane += hi - lo


def valid(lo, size):
    at = lo + lax.broadcasted_iota(jnp.int32, (size, 128), 0)
    ok = (at >= STRIDE) & (at < STRIDE + OWN)
    for row in range(1, 7):
        gap = STRIDE * row + W
        if lo < gap + STRIDE - W and gap < lo + size:
            ok = ok & ((at < gap) | (at >= gap + STRIDE - W))
    return ok


def moments(pt_ref, weight):
    lanes = weight.shape[1]
    pilot = None
    s1 = s2 = jnp.zeros((8, lanes), jnp.float32)
    for g in range(FRAMES):
        for lo, size in K1_CHUNKS:
            h = lax.dot_general(
                pt_ref[max(g, 2) * TAPS : (g + 3) * TAPS, lo : lo + size],
                weight[max(2 - g, 0) * TAPS :],
                (((0,), (0,)), ((), ())),
                preferred_element_type=jnp.float32,
            )
            ok = jnp.concatenate([valid(lo, size)] * (lanes // 128), axis=1)
            if pilot is None:
                cells = sum(lo <= STRIDE * row + col < lo + size for row in range(1, 7) for col in range(W))
                pilot = jnp.sum(jnp.where(ok, h, 0.0), axis=0, keepdims=True) * (1.0 / cells)
            d = jnp.where(ok, h - pilot, 0.0).reshape(size // 8, 8, lanes)
            s1 = s1 + jnp.sum(d, axis=0)
            s2 = s2 + jnp.sum(d * d, axis=0)
    s1 = jnp.sum(s1, axis=0, keepdims=True)
    s2 = jnp.sum(s2, axis=0, keepdims=True)
    d = s1 / (FRAMES * CELLS)
    return pilot + d, s2 - s1 * d


def k1p(x_ref, held_ref, side_ref, pt_ref, near_ref):
    pt_ref[: 2 * TAPS, :] = jnp.zeros((2 * TAPS, SPAN), jnp.bfloat16)
    for f in range(FRAMES):
        for b in range(3):
            for e in range(3):
                at = (f + 2) * TAPS + (3 * b + e) * 16
                lane = LEAD + STRIDE * b + e - 1
                pt_ref[at : at + 16, :] = x_ref[16 * f : 16 * f + 16, lane : lane + SPAN]
    mean, squares = moments(pt_ref, jnp.concatenate([held_ref[:TAPROWS], side_ref[:TAPROWS]], axis=1))
    for i in range(2):
        near_ref[i : i + 1] = mean[:, 128 * i : 128 * (i + 1)]
        near_ref[2 + i : 3 + i] = squares[:, 128 * i : 128 * (i + 1)]
    near_ref[4:] = jnp.zeros((4, 128), jnp.float32)


def k1q(pt_ref, near_ref, held_ref, mine_ref, other_ref, wall_ref, st_ref):
    c, core = lax.axis_index("ch"), lax.rem(lax.axis_index("row"), 2)
    side, side_x, far = (lax.rem(c + i, 4) for i in (1 + 2 * core, 3 - 2 * core, 2))
    wall_ref[c] = held_ref[...]
    wall_ref[side] = mine_ref[:HELD, :]
    wall_ref[side_x] = other_ref[:HELD, :]
    wall_ref[far, pl.ds(pl.multiple_of(core * HALF, 16), HALF), :] = mine_ref[HELD:, :]
    wall_ref[far, pl.ds(pl.multiple_of((1 - core) * HALF, 16), HALF), :] = other_ref[HELD:, :]
    mean, squares = moments(pt_ref, jnp.concatenate([other_ref[:TAPROWS], wall_ref[far][:TAPROWS]], axis=1))

    def send(at, v):
        st_ref[:, pl.ds(at, 1), :] = jnp.broadcast_to(v[None], (16, 1, 128))

    for at, m, q in (
        (c, near_ref[0:1], near_ref[2:3]),
        (side, near_ref[1:2], near_ref[3:4]),
        (side_x, mean[:, :128], squares[:, :128]),
        (far, mean[:, 128:], squares[:, 128:]),
    ):
        send(at, m)
        send(4 + at, q)


def k2(pt_ref, wall_ref, st_ref, w2_hbm, mix_ref, so_ref, a_ref, w2_ref, y_ref, sem):
    copy = pltpu.make_async_copy(w2_hbm, w2_ref, sem)
    copy.start()
    f, r = lax.axis_index("frm"), lax.axis_index("row")
    weight = jnp.concatenate([wall_ref[j, :TAPROWS, :] for j in range(4)], axis=1)

    def spread3(at):
        rows = [wall_ref[j, TAPROWS:, :].astype(jnp.float32)[at : at + 3] for j in range(4)]
        return jnp.concatenate([jnp.sum(r, axis=0, keepdims=True) for r in rows], axis=1)

    n = FRAMES * CELLS
    st = st_ref[...]
    sums = jnp.sum(st, axis=0)
    means = sums[:4] * (1.0 / 16)
    off = st[:, :4, :] - means[None]
    spread = jnp.sum(off * off, axis=0)
    mean, var = group_moments(eight(means), eight((sums[4:] * (1.0 / n) + spread) * (1.0 / 16)))
    inverse = lax.rsqrt(var + EPSILON)

    def wide(v):
        return jnp.concatenate([v[j : j + 1] for j in range(4)], axis=1)

    mean, scale, shift = wide(mean), 0.5 * wide(inverse) * spread3(0), 0.5 * spread3(3)

    a_ref[0:16, :] = jnp.zeros((16, 3 * CH), jnp.bfloat16)
    a_ref[16 + SPAN :, :] = jnp.zeros((16, 3 * CH), jnp.bfloat16)
    for k in range(3):
        g = f - 2 + k

        @pl.when(g >= 0)
        def _():
            at = pl.multiple_of(g * TAPS, 16)
            for lo, size in CHUNKS:
                h = lax.dot_general(
                    pt_ref[pl.ds(at, 3 * TAPS), lo : lo + size],
                    weight,
                    (((0,), (0,)), ((), ())),
                    preferred_element_type=jnp.float32,
                )
                u = silu_of_twice((h - mean) * scale + shift)
                a_ref[16 + lo : 16 + lo + size, k * CH : (k + 1) * CH] = u.astype(jnp.bfloat16)

        @pl.when(g < 0)
        def _():
            a_ref[16 : 16 + SPAN, k * CH : (k + 1) * CH] = jnp.zeros((SPAN, CH), jnp.bfloat16)

    keep = lax.broadcasted_iota(jnp.int32, (16, 3 * CH), 0) < 10
    for row in range(8):
        at = 16 + STRIDE * row + 160
        a_ref[at : at + 16, :] = jnp.where(keep, a_ref[at : at + 16, :], 0).astype(jnp.bfloat16)

    @pl.when(r == 0)
    def _():
        a_ref[16 : 16 + STRIDE, :] = jnp.zeros((STRIDE, 3 * CH), jnp.bfloat16)

    @pl.when(r == 15)
    def _():
        a_ref[16 + 7 * STRIDE : 16 + SPAN, :] = jnp.zeros((STRIDE, 3 * CH), jnp.bfloat16)

    copy.wait()

    def product(start, rows, *taps):
        kernel = jnp.concatenate(
            [jnp.concatenate([w2_ref[9 * a + 3 * b + e] for a in range(3)], axis=0) for b, e in taps], axis=1
        )
        y_ref[:rows, : 128 * len(taps)] = jnp.dot(
            a_ref[start : start + rows, :], kernel, preferred_element_type=jnp.float32
        )

    for b in range(3):
        product(STRIDE * b, OWN + 32, (b, 0), (b, 2))
        part = y_ref[15 : 15 + OWN, :128] + y_ref[17 : 17 + OWN, 128:]
        mix_ref[...] = part if b == 0 else mix_ref[...] + part
    product(16, OWN + STRIDE, (0, 1), (1, 1))
    mix_ref[...] += y_ref[0:OWN, :128] + y_ref[STRIDE : STRIDE + OWN, 128:]
    product(16 + 2 * STRIDE, OWN, (2, 1))
    v = (mix_ref[...] + y_ref[0:OWN, :128]).reshape(ROWS, STRIDE, 128)
    mix_ref[...] = v.reshape(OWN, 128)
    ok = lax.broadcasted_iota(jnp.int32, (ROWS, STRIDE, 128), 1) < W
    total = jnp.sum(jnp.sum(jnp.where(ok, v, 0.0), axis=0), axis=0, keepdims=True)
    centre = total / CELLS
    off = jnp.where(ok, v - centre[None], 0.0)
    squares = jnp.sum(jnp.sum(off * off, axis=0), axis=0, keepdims=True)
    so_ref[:, 0:1, :] = jnp.broadcast_to(centre[None], (64, 1, 128))
    so_ref[:, 1:2, :] = jnp.broadcast_to(squares[None], (64, 1, 128))


def k3(mix_ref, st_ref, par_ref, out_ref):
    st = st_ref[...]
    sums = jnp.sum(st, axis=0)
    means = sums * (1.0 / 64)
    off = st - means[None]
    spread = jnp.sum(off * off, axis=0)
    var = (sums[1:2] * (1.0 / CELLS) + spread[0:1]) * (1.0 / 64)
    mean, var = group_moments(eight(means[0:1]), eight(var))
    mean = mean[:1]
    scale = 0.5 * lax.rsqrt(var[:1] + EPSILON) * par_ref[0]
    shift = 0.5 * par_ref[1]
    for row in range(ROWS):
        v = mix_ref[STRIDE * row : STRIDE * (row + 1), :]
        u = silu_of_twice((v - mean) * scale + shift)
        out_ref[0, row] = u[:W].astype(jnp.bfloat16)


def shape(dims, kind):
    return jax.ShapeDtypeStruct(dims, kind)


INHBM = pl.BlockSpec(memory_space=pltpu.HBM)
INVMEM = pl.BlockSpec(memory_space=pltpu.VMEM)


def call_k0(*arrays):
    return pl.pallas_call(
        k0,
        out_shape=(
            shape((16, C_LAT, 255), jnp.bfloat16),
            shape((HELD, 128), jnp.bfloat16),
            shape((HALF, 128), jnp.bfloat16),
            shape((2, 1, 128), jnp.float32),
        ),
        in_specs=[INHBM] * 6,
        out_specs=(INVMEM,) * 4,
        scratch_shapes=[
            pltpu.VMEM((C_LAT, 255), jnp.bfloat16),
            pltpu.VMEM((2, 1, 128), jnp.float32),
            pltpu.SemaphoreType.DMA((6,)),
        ],
        compiler_params=pltpu.CompilerParams(vmem_limit_bytes=VMEM),
        name="k0",
    )(*[pltpu.with_memory_space_constraint(v, pltpu.HBM) for v in arrays])


def call(kernel, name, outs, *arrays):
    return pl.pallas_call(
        kernel,
        out_shape=tuple(shape(*out) for out in outs),
        in_specs=[INVMEM] * len(arrays),
        out_specs=(INVMEM,) * len(outs),
        compiler_params=pltpu.CompilerParams(vmem_limit_bytes=VMEM),
        name=name,
    )(*arrays)


def call_k2(pt, wall, st, w2):
    return pl.pallas_call(
        k2,
        out_shape=(shape((OWN, 128), jnp.float32), shape((64, 2, 128), jnp.float32)),
        in_specs=[INVMEM] * 3 + [INHBM],
        out_specs=(INVMEM,) * 2,
        scratch_shapes=[
            pltpu.VMEM((SPAN + 32, 3 * CH), jnp.bfloat16),
            pltpu.VMEM((27, CH, 128), jnp.bfloat16),
            pltpu.VMEM((SPAN, 256), jnp.float32),
            pltpu.SemaphoreType.DMA,
        ],
        compiler_params=pltpu.CompilerParams(vmem_limit_bytes=VMEM),
        name="k2",
    )(pt, wall, st, pltpu.with_memory_space_constraint(w2, pltpu.HBM))


def call_k3(mix, st, par):
    return pl.pallas_call(
        k3,
        out_shape=shape((1, ROWS, W, 128), jnp.bfloat16),
        in_specs=[INVMEM] * 3,
        out_specs=INVMEM,
        compiler_params=pltpu.CompilerParams(vmem_limit_bytes=VMEM),
        name="k3",
    )(mix, st, par)


def per_device(latents, in_weight, in_gain, in_shift, mid_weight, mid_gain, mid_shift):
    params = [v.reshape(1, 128) for v in (in_gain, in_shift, mid_gain, mid_shift)]
    payload, held, half, par = call_k0(latents.T, in_weight.reshape(TAPROWS, 128), *params)
    g = lax.all_to_all(payload, ("frm", "ch"), 0, 0)
    sides = [(4 * i + (j + 1 + 2 * (i % 2)) % 4, 4 * i + j) for i in range(16) for j in range(4)]
    side = lax.ppermute(held, ("row", "ch"), sides)
    fars = [(4 * (i ^ 8) + (j + 2) % 4, 4 * i + j) for i in range(16) for j in range(4)]
    far = lax.ppermute(half, ("row", "ch"), fars)
    cores = [(i, i ^ 1) for i in range(16)]
    edge = ((16 * FRAMES, 384), jnp.bfloat16)
    to_next, to_mate = call(k1t, "k1t", [edge] * 2, g)
    to_next = lax.ppermute(to_next, "row", [(i, i + 2 * (i % 2) - 1) for i in range(1, 15)])
    to_mate = lax.ppermute(to_mate, "row", cores)
    both = ((HELD + HALF, 128), jnp.bfloat16)
    mine, x = call(k1w, "k1w", [both, ((16 * FRAMES, XLANES), jnp.bfloat16)], g, side, far, to_next, to_mate)
    other = lax.ppermute(mine, "row", cores)
    pt, near = call(k1p, "k1p", [((6 * TAPS, SPAN), jnp.bfloat16), ((8, 128), jnp.float32)], x, held, side)
    outs = [((4, HELD, 128), jnp.bfloat16), ((16, 8, 128), jnp.float32)]
    wall, st = call(k1q, "k1q", outs, pt, near, held, mine, other)
    st = lax.all_to_all(st, "row", 0, 0)
    mix, st = call_k2(pt, wall, st, mid_weight)
    st = lax.all_to_all(st, ("frm", "row"), 0, 0)
    return call_k3(mix, st, par)


def solution(mesh):
    return jax.shard_map(
        per_device,
        mesh=mesh,
        in_specs=(
            P(("frm", "row", "ch"), None),
            P(None, None, "ch"),
            P("ch"),
            P("ch"),
            P(None, None, "ch"),
            P("ch"),
            P("ch"),
        ),
        out_specs=P("frm", "row", None, "ch"),
        check_vma=False,
    )
```

```python
import jax
import jax.numpy as jnp
from jax import lax
from jax.experimental import pallas as pl
from jax.experimental.pallas import tpu as pltpu
from jax.sharding import PartitionSpec as P

CH = 512
GROUP = 16
W = 170
ROWS = 6
C_LAT = 16
FRAMES = 4
EPSILON = 1e-06

STRIDE = 176
SPAN = 8 * STRIDE
OWN = ROWS * STRIDE
TAPS = 9 * C_LAT
LEAD = 128
XLANES = 2048
MID = (384, 640)
SIDES = 384
CELLS = ROWS * W
TAPROWS = 27 * C_LAT
HELD = 448
HALF = HELD // 2
VMEM = 48 * 1024 * 1024


def silu_of_twice(half):
    return half + half * jnp.tanh(half)


def group_mean(v):
    r = lax.broadcasted_iota(jnp.int32, (128, 128), 0) // GROUP
    c = lax.broadcasted_iota(jnp.int32, (128, 128), 1) // GROUP
    same = jnp.where(r == c, 1.0 / GROUP, 0.0).astype(jnp.bfloat16)
    high = v.astype(jnp.bfloat16).astype(jnp.float32)
    mid = (v - high).astype(jnp.bfloat16).astype(jnp.float32)
    low = v - high - mid
    y = jnp.dot(
        jnp.concatenate([high, mid, low], axis=0).astype(jnp.bfloat16),
        same,
        preferred_element_type=jnp.float32,
    )
    return y[0:8] + y[8:16] + y[16:24]


def eight(v):
    return jnp.concatenate([v, jnp.zeros((8 - v.shape[0], 128), jnp.float32)], axis=0)


def group_moments(mean, var):
    mean_g = group_mean(mean)
    off = mean - mean_g
    return mean_g, group_mean(var + off * off)


def parts3(v):
    high = v.astype(jnp.bfloat16).astype(jnp.float32)
    mid = (v - high).astype(jnp.bfloat16).astype(jnp.float32)
    return [high, mid, v - high - mid]


def k0(tokens_hbm, out_ref, tokens_ref, sem):
    copy = pltpu.make_async_copy(tokens_hbm, tokens_ref, sem)
    copy.start()
    copy.wait()
    out_ref[...] = jnp.broadcast_to(tokens_ref[...][None], (16, C_LAT, 255))


def k0w(w_hbm, p0, p1, p2, p3, held_ref, half_ref, par_ref, in_ref, sems):
    copies = [
        pltpu.make_async_copy(w_hbm, held_ref.at[:TAPROWS], sems.at[0]),
        pltpu.make_async_copy(p0, in_ref.at[0], sems.at[1]),
        pltpu.make_async_copy(p1, in_ref.at[1], sems.at[2]),
        pltpu.make_async_copy(p2, par_ref.at[0], sems.at[3]),
        pltpu.make_async_copy(p3, par_ref.at[1], sems.at[4]),
    ]
    for copy in copies:
        copy.start()
    for copy in copies:
        copy.wait()
    rows = parts3(in_ref[0]) + parts3(in_ref[1]) + [jnp.zeros((10, 128), jnp.float32)]
    held_ref[TAPROWS:, :] = jnp.concatenate(rows, axis=0).astype(jnp.bfloat16)
    start = pl.multiple_of(lax.rem(lax.axis_index("row"), 2) * HALF, 16)
    half_ref[...] = held_ref[pl.ds(start, HALF), :]


def first_rows(g_ref, f):
    return ((0, g_ref[4 * f, :, :170]), (176, g_ref[4 * f, :, 170:255]), (261, g_ref[4 * f + 1, :, :85]))


def last_rows(g_ref, f):
    return ((0, g_ref[4 * f + 2, :, 170:255]), (85, g_ref[4 * f + 3, :, :85]), (176, g_ref[4 * f + 3, :, 85:255]))


def write_edge(rows, g_ref, out_ref):
    for f in range(FRAMES):
        for lane, v in rows(g_ref, f):
            out_ref[16 * f : 16 * f + 16, lane : lane + v.shape[1]] = v


def k1t(g_ref, next_ref, mate_ref):
    next_ref[...] = jnp.zeros_like(next_ref)
    mate_ref[...] = jnp.zeros_like(mate_ref)
    core = lax.rem(lax.axis_index("row"), 2)

    @pl.when(core == 0)
    def _():
        write_edge(first_rows, g_ref, next_ref)
        write_edge(last_rows, g_ref, mate_ref)

    @pl.when(core == 1)
    def _():
        write_edge(last_rows, g_ref, next_ref)
        write_edge(first_rows, g_ref, mate_ref)


def k1i(g_ref, held_ref, side_ref, x_ref, mid_ref, acc_ref):
    x_ref[...] = jnp.zeros_like(x_ref)
    plan = (
        ((0, 0, 170),),
        ((0, 170, 255), (1, 0, 85)),
        ((1, 85, 255),),
        ((2, 0, 170),),
        ((2, 170, 255), (3, 0, 85)),
        ((3, 85, 255),),
    )
    for f in range(FRAMES):
        at = slice(16 * f, 16 * f + 16)
        for row, parts in enumerate(plan):
            lane = LEAD + STRIDE * (row + 2)
            for j, lo, hi in parts:
                x_ref[at, lane : lane + hi - lo] = g_ref[4 * f + j, :, lo:hi]
                lane += hi - lo
    mid_ref[: 2 * TAPS, :] = jnp.zeros((2 * TAPS, MID[1]), jnp.bfloat16)
    patches(x_ref, mid_ref, 0, *MID)
    weight = jnp.concatenate([held_ref[:TAPROWS], side_ref[:TAPROWS]], axis=1)
    pilot, s1, s2 = moments(weight, ((mid_ref, 0, *MID),))
    acc_ref[0:8] = s1
    acc_ref[8:16] = s2
    acc_ref[16:24] = jnp.broadcast_to(pilot, (8, 256))


def k1w(x_in_ref, side_ref, far_ref, next_ref, mate_ref, both_ref, x_ref):
    both_ref[:HELD] = side_ref[...]
    both_ref[HELD:] = far_ref[...]
    x_ref[...] = x_in_ref[...]
    core = lax.rem(lax.axis_index("row"), 2)

    def edges(above_ref, below_ref):
        x_ref[:, LEAD : LEAD + 2 * STRIDE] = above_ref[:, : 2 * STRIDE]
        x_ref[:, LEAD + 8 * STRIDE : LEAD + 10 * STRIDE] = below_ref[:, : 2 * STRIDE]

    @pl.when(core == 0)
    def _():
        edges(next_ref, mate_ref)

    @pl.when(core == 1)
    def _():
        edges(mate_ref, next_ref)


def patches(x_ref, out_ref, lane, lo, size):
    for f in range(FRAMES):
        for b in range(3):
            for e in range(3):
                at = (f + 2) * TAPS + (3 * b + e) * 16
                start = LEAD + lo + STRIDE * b + e - 1
                out_ref[at : at + 16, lane : lane + size] = x_ref[16 * f : 16 * f + 16, start : start + size]


def valid(lo, size):
    at = lo + lax.broadcasted_iota(jnp.int32, (size, 128), 0)
    ok = (at >= STRIDE) & (at < STRIDE + OWN)
    for row in range(1, 7):
        gap = STRIDE * row + W
        if lo < gap + STRIDE - W and gap < lo + size:
            ok = ok & ((at < gap) | (at >= gap + STRIDE - W))
    return ok


def moments(weight, chunks, carry=None):
    lanes = weight.shape[1]
    zero = jnp.zeros((8, lanes), jnp.float32)
    pilot, s1, s2 = carry or (None, zero, zero)
    for g in range(FRAMES):
        for ref, lane, lo, size in chunks:
            h = lax.dot_general(
                ref[max(g, 2) * TAPS : (g + 3) * TAPS, lane : lane + size],
                weight[max(2 - g, 0) * TAPS :],
                (((0,), (0,)), ((), ())),
                preferred_element_type=jnp.float32,
            )
            ok = jnp.concatenate([valid(lo, size)] * (lanes // 128), axis=1)
            if pilot is None:
                cells = sum(lo <= STRIDE * row + col < lo + size for row in range(1, 7) for col in range(W))
                pilot = jnp.sum(jnp.where(ok, h, 0.0), axis=0, keepdims=True) * (1.0 / cells)
            d = jnp.where(ok, h - pilot, 0.0).reshape(size // 8, 8, lanes)
            s1 = s1 + jnp.sum(d, axis=0)
            s2 = s2 + jnp.sum(d * d, axis=0)
    return pilot, s1, s2


def centred(pilot, s1, s2):
    s1 = jnp.sum(s1, axis=0, keepdims=True)
    s2 = jnp.sum(s2, axis=0, keepdims=True)
    d = s1 / (FRAMES * CELLS)
    return pilot + d, s2 - s1 * d


def outer(ref):
    return ((ref, 128, 128, 256), (ref, SIDES, SPAN - SIDES, 256))


def k1p(x_ref, held_ref, side_ref, acc_ref, out_ref, near_ref):
    out_ref[: 2 * TAPS, :] = jnp.zeros((2 * TAPS, 2 * SIDES), jnp.bfloat16)
    patches(x_ref, out_ref, 0, 0, SIDES)
    patches(x_ref, out_ref, SIDES, SPAN - SIDES, SIDES)
    weight = jnp.concatenate([held_ref[:TAPROWS], side_ref[:TAPROWS]], axis=1)
    mean, squares = centred(*moments(weight, outer(out_ref), (acc_ref[16:17], acc_ref[0:8], acc_ref[8:16])))
    for i in range(2):
        near_ref[i : i + 1] = mean[:, 128 * i : 128 * (i + 1)]
        near_ref[2 + i : 3 + i] = squares[:, 128 * i : 128 * (i + 1)]
    near_ref[4:] = jnp.zeros((4, 128), jnp.float32)


def k1q(mid_ref, out_ref, near_ref, held_ref, mine_ref, other_ref, wall_ref, st_ref):
    c, core = lax.axis_index("ch"), lax.rem(lax.axis_index("row"), 2)
    side, side_x, far = (lax.rem(c + i, 4) for i in (1 + 2 * core, 3 - 2 * core, 2))
    wall_ref[c] = held_ref[...]
    wall_ref[side] = mine_ref[:HELD, :]
    wall_ref[side_x] = other_ref[:HELD, :]
    wall_ref[far, pl.ds(pl.multiple_of(core * HALF, 16), HALF), :] = mine_ref[HELD:, :]
    wall_ref[far, pl.ds(pl.multiple_of((1 - core) * HALF, 16), HALF), :] = other_ref[HELD:, :]
    weight = jnp.concatenate([other_ref[:TAPROWS], wall_ref[far][:TAPROWS]], axis=1)
    mean, squares = centred(*moments(weight, ((mid_ref, 0, *MID), *outer(out_ref))))

    def send(at, v):
        st_ref[:, pl.ds(at, 1), :] = jnp.broadcast_to(v[None], (16, 1, 128))

    for at, m, q in (
        (c, near_ref[0:1], near_ref[2:3]),
        (side, near_ref[1:2], near_ref[3:4]),
        (side_x, mean[:, :128], squares[:, :128]),
        (far, mean[:, 128:], squares[:, 128:]),
    ):
        send(at, m)
        send(4 + at, q)


def k2(mid_ref, out_ref, wall_ref, st_ref, w2_hbm, mix_ref, so_ref, a_ref, w2_ref, y_ref, sem):
    copy = pltpu.make_async_copy(w2_hbm, w2_ref, sem)
    copy.start()
    f, r = lax.axis_index("frm"), lax.axis_index("row")
    weight = jnp.concatenate([wall_ref[j, :TAPROWS, :] for j in range(4)], axis=1)

    def spread3(at):
        rows = [wall_ref[j, TAPROWS:, :].astype(jnp.float32)[at : at + 3] for j in range(4)]
        return jnp.concatenate([jnp.sum(r, axis=0, keepdims=True) for r in rows], axis=1)

    n = FRAMES * CELLS
    st = st_ref[...]
    sums = jnp.sum(st, axis=0)
    means = sums[:4] * (1.0 / 16)
    off = st[:, :4, :] - means[None]
    spread = jnp.sum(off * off, axis=0)
    mean, var = group_moments(eight(means), eight((sums[4:] * (1.0 / n) + spread) * (1.0 / 16)))
    inverse = lax.rsqrt(var + EPSILON)

    def wide(v):
        return jnp.concatenate([v[j : j + 1] for j in range(4)], axis=1)

    mean, scale, shift = wide(mean), 0.5 * wide(inverse) * spread3(0), 0.5 * spread3(3)

    a_ref[0:16, :] = jnp.zeros((16, 3 * CH), jnp.bfloat16)
    a_ref[16 + SPAN :, :] = jnp.zeros((16, 3 * CH), jnp.bfloat16)
    for k in range(3):
        g = f - 2 + k

        @pl.when(g >= 0)
        def _():
            at = pl.multiple_of(g * TAPS, 16)
            for ref, lane, lo, size in (
                (out_ref, 0, 0, SIDES),
                (mid_ref, 0, *MID),
                (out_ref, SIDES, SPAN - SIDES, SIDES),
            ):
                h = lax.dot_general(
                    ref[pl.ds(at, 3 * TAPS), lane : lane + size],
                    weight,
                    (((0,), (0,)), ((), ())),
                    preferred_element_type=jnp.float32,
                )
                u = silu_of_twice((h - mean) * scale + shift)
                a_ref[16 + lo : 16 + lo + size, k * CH : (k + 1) * CH] = u.astype(jnp.bfloat16)

        @pl.when(g < 0)
        def _():
            a_ref[16 : 16 + SPAN, k * CH : (k + 1) * CH] = jnp.zeros((SPAN, CH), jnp.bfloat16)

    keep = lax.broadcasted_iota(jnp.int32, (16, 3 * CH), 0) < 10
    for row in range(8):
        at = 16 + STRIDE * row + 160
        a_ref[at : at + 16, :] = jnp.where(keep, a_ref[at : at + 16, :], 0).astype(jnp.bfloat16)

    @pl.when(r == 0)
    def _():
        a_ref[16 : 16 + STRIDE, :] = jnp.zeros((STRIDE, 3 * CH), jnp.bfloat16)

    @pl.when(r == 15)
    def _():
        a_ref[16 + 7 * STRIDE : 16 + SPAN, :] = jnp.zeros((STRIDE, 3 * CH), jnp.bfloat16)

    copy.wait()

    def product(start, rows, *taps):
        kernel = jnp.concatenate(
            [jnp.concatenate([w2_ref[9 * a + 3 * b + e] for a in range(3)], axis=0) for b, e in taps], axis=1
        )
        y_ref[:rows, : 128 * len(taps)] = jnp.dot(
            a_ref[start : start + rows, :], kernel, preferred_element_type=jnp.float32
        )

    for b in range(3):
        product(STRIDE * b, OWN + 32, (b, 0), (b, 2))
        part = y_ref[15 : 15 + OWN, :128] + y_ref[17 : 17 + OWN, 128:]
        mix_ref[...] = part if b == 0 else mix_ref[...] + part
    product(16, OWN + STRIDE, (0, 1), (1, 1))
    mix_ref[...] += y_ref[0:OWN, :128] + y_ref[STRIDE : STRIDE + OWN, 128:]
    product(16 + 2 * STRIDE, OWN, (2, 1))
    v = (mix_ref[...] + y_ref[0:OWN, :128]).reshape(ROWS, STRIDE, 128)
    mix_ref[...] = v.reshape(OWN, 128)
    ok = lax.broadcasted_iota(jnp.int32, (ROWS, STRIDE, 128), 1) < W
    total = jnp.sum(jnp.sum(jnp.where(ok, v, 0.0), axis=0), axis=0, keepdims=True)
    centre = total / CELLS
    off = jnp.where(ok, v - centre[None], 0.0)
    squares = jnp.sum(jnp.sum(off * off, axis=0), axis=0, keepdims=True)
    so_ref[:, 0:1, :] = jnp.broadcast_to(centre[None], (64, 1, 128))
    so_ref[:, 1:2, :] = jnp.broadcast_to(squares[None], (64, 1, 128))


def k3(mix_ref, st_ref, par_ref, out_ref):
    st = st_ref[...]
    sums = jnp.sum(st, axis=0)
    means = sums * (1.0 / 64)
    off = st - means[None]
    spread = jnp.sum(off * off, axis=0)
    var = (sums[1:2] * (1.0 / CELLS) + spread[0:1]) * (1.0 / 64)
    mean, var = group_moments(eight(means[0:1]), eight(var))
    mean = mean[:1]
    scale = 0.5 * lax.rsqrt(var[:1] + EPSILON) * par_ref[0]
    shift = 0.5 * par_ref[1]
    for row in range(ROWS):
        v = mix_ref[STRIDE * row : STRIDE * (row + 1), :]
        u = silu_of_twice((v - mean) * scale + shift)
        out_ref[0, row] = u[:W].astype(jnp.bfloat16)


def shape(dims, kind):
    return jax.ShapeDtypeStruct(dims, kind)


INHBM = pl.BlockSpec(memory_space=pltpu.HBM)
INVMEM = pl.BlockSpec(memory_space=pltpu.VMEM)


def in_hbm(v):
    return pltpu.with_memory_space_constraint(v, pltpu.HBM)


def call_k0(tokens):
    return pl.pallas_call(
        k0,
        out_shape=shape((16, C_LAT, 255), jnp.bfloat16),
        in_specs=[INHBM],
        out_specs=INVMEM,
        scratch_shapes=[pltpu.VMEM((C_LAT, 255), jnp.bfloat16), pltpu.SemaphoreType.DMA],
        compiler_params=pltpu.CompilerParams(vmem_limit_bytes=VMEM),
        name="k0",
    )(in_hbm(tokens))


def call_k0w(*arrays):
    return pl.pallas_call(
        k0w,
        out_shape=(
            shape((HELD, 128), jnp.bfloat16),
            shape((HALF, 128), jnp.bfloat16),
            shape((2, 1, 128), jnp.float32),
        ),
        in_specs=[INHBM] * 5,
        out_specs=(INVMEM,) * 3,
        scratch_shapes=[pltpu.VMEM((2, 1, 128), jnp.float32), pltpu.SemaphoreType.DMA((5,))],
        compiler_params=pltpu.CompilerParams(vmem_limit_bytes=VMEM),
        name="k0w",
    )(*[in_hbm(v) for v in arrays])


def call(kernel, name, outs, *arrays):
    return pl.pallas_call(
        kernel,
        out_shape=tuple(shape(*out) for out in outs),
        in_specs=[INVMEM] * len(arrays),
        out_specs=(INVMEM,) * len(outs),
        compiler_params=pltpu.CompilerParams(vmem_limit_bytes=VMEM),
        name=name,
    )(*arrays)


def call_k2(*arrays):
    return pl.pallas_call(
        k2,
        out_shape=(shape((OWN, 128), jnp.float32), shape((64, 2, 128), jnp.float32)),
        in_specs=[INVMEM] * 4 + [INHBM],
        out_specs=(INVMEM,) * 2,
        scratch_shapes=[
            pltpu.VMEM((SPAN + 32, 3 * CH), jnp.bfloat16),
            pltpu.VMEM((27, CH, 128), jnp.bfloat16),
            pltpu.VMEM((SPAN, 256), jnp.float32),
            pltpu.SemaphoreType.DMA,
        ],
        compiler_params=pltpu.CompilerParams(vmem_limit_bytes=VMEM),
        name="k2",
    )(*arrays[:4], in_hbm(arrays[4]))


def call_k3(mix, st, par):
    return pl.pallas_call(
        k3,
        out_shape=shape((1, ROWS, W, 128), jnp.bfloat16),
        in_specs=[INVMEM] * 3,
        out_specs=INVMEM,
        compiler_params=pltpu.CompilerParams(vmem_limit_bytes=VMEM),
        name="k3",
    )(mix, st, par)


def per_device(latents, in_weight, in_gain, in_shift, mid_weight, mid_gain, mid_shift):
    params = [v.reshape(1, 128) for v in (in_gain, in_shift, mid_gain, mid_shift)]
    g = lax.all_to_all(call_k0(latents.T), ("frm", "ch"), 0, 0)
    held, half, par = call_k0w(in_weight.reshape(TAPROWS, 128), *params)
    sides = [(4 * i + (j + 1 + 2 * (i % 2)) % 4, 4 * i + j) for i in range(16) for j in range(4)]
    side = lax.ppermute(held, ("row", "ch"), sides)
    fars = [(4 * (i ^ 8) + (j + 2) % 4, 4 * i + j) for i in range(16) for j in range(4)]
    far = lax.ppermute(half, ("row", "ch"), fars)
    cores = [(i, i ^ 1) for i in range(16)]
    edge = ((16 * FRAMES, 384), jnp.bfloat16)
    to_next, to_mate = call(k1t, "k1t", [edge] * 2, g)
    to_next = lax.ppermute(to_next, "row", [(i, i + 2 * (i % 2) - 1) for i in range(1, 15)])
    to_mate = lax.ppermute(to_mate, "row", cores)
    own = ((16 * FRAMES, XLANES), jnp.bfloat16)
    outs = [own, ((6 * TAPS, MID[1]), jnp.bfloat16), ((24, 256), jnp.float32)]
    x, mid, acc = call(k1i, "k1i", outs, g, held, side)
    mine, x = call(k1w, "k1w", [((HELD + HALF, 128), jnp.bfloat16), own], x, side, far, to_next, to_mate)
    other = lax.ppermute(mine, "row", cores)
    outs = [((6 * TAPS, 2 * SIDES), jnp.bfloat16), ((8, 128), jnp.float32)]
    outer_patches, near = call(k1p, "k1p", outs, x, held, side, acc)
    outs = [((4, HELD, 128), jnp.bfloat16), ((16, 8, 128), jnp.float32)]
    wall, st = call(k1q, "k1q", outs, mid, outer_patches, near, held, mine, other)
    st = lax.all_to_all(st, "row", 0, 0)
    mix, st = call_k2(mid, outer_patches, wall, st, mid_weight)
    st = lax.all_to_all(st, ("frm", "row"), 0, 0)
    return call_k3(mix, st, par)


def solution(mesh):
    return jax.shard_map(
        per_device,
        mesh=mesh,
        in_specs=(
            P(("frm", "row", "ch"), None),
            P(None, None, "ch"),
            P("ch"),
            P("ch"),
            P(None, None, "ch"),
            P("ch"),
            P("ch"),
        ),
        out_specs=P("frm", "row", None, "ch"),
        check_vma=False,
    )
```

```python
import jax
import jax.numpy as jnp
from jax import lax
from jax.experimental import pallas as pl
from jax.experimental.pallas import tpu as pltpu
from jax.sharding import PartitionSpec as P

CH = 512
GROUP = 16
W = 170
ROWS = 6
C_LAT = 16
FRAMES = 4
EPSILON = 1e-06

STRIDE = 176
SPAN = 8 * STRIDE
OWN = ROWS * STRIDE
TAPS = 9 * C_LAT
LEAD = 128
XLANES = 2048
MID = (384, 640)
SIDES = 384
CELLS = ROWS * W
TAPROWS = 27 * C_LAT
HELD = 448
HALF = HELD // 2
VMEM = 48 * 1024 * 1024


def silu_of_twice(half):
    return half + half * jnp.tanh(half)


def group_mean(v):
    r = lax.broadcasted_iota(jnp.int32, (128, 128), 0) // GROUP
    c = lax.broadcasted_iota(jnp.int32, (128, 128), 1) // GROUP
    same = jnp.where(r == c, 1.0 / GROUP, 0.0).astype(jnp.bfloat16)
    high = v.astype(jnp.bfloat16).astype(jnp.float32)
    mid = (v - high).astype(jnp.bfloat16).astype(jnp.float32)
    low = v - high - mid
    y = jnp.dot(
        jnp.concatenate([high, mid, low], axis=0).astype(jnp.bfloat16),
        same,
        preferred_element_type=jnp.float32,
    )
    return y[0:8] + y[8:16] + y[16:24]


def eight(v):
    return jnp.concatenate([v, jnp.zeros((8 - v.shape[0], 128), jnp.float32)], axis=0)


def group_moments(mean, var):
    mean_g = group_mean(mean)
    off = mean - mean_g
    return mean_g, group_mean(var + off * off)


def parts3(v):
    high = v.astype(jnp.bfloat16).astype(jnp.float32)
    mid = (v - high).astype(jnp.bfloat16).astype(jnp.float32)
    return [high, mid, v - high - mid]


def k0(tokens_hbm, out_ref, tokens_ref, sem):
    copy = pltpu.make_async_copy(tokens_hbm, tokens_ref, sem)
    copy.start()
    copy.wait()
    out_ref[...] = jnp.broadcast_to(tokens_ref[...][None], (16, C_LAT, 255))


def k0w(w_hbm, p0, p1, p2, p3, held_ref, half_ref, par_ref, in_ref, sems):
    copies = [
        pltpu.make_async_copy(w_hbm, held_ref.at[:TAPROWS], sems.at[0]),
        pltpu.make_async_copy(p0, in_ref.at[0], sems.at[1]),
        pltpu.make_async_copy(p1, in_ref.at[1], sems.at[2]),
        pltpu.make_async_copy(p2, par_ref.at[0], sems.at[3]),
        pltpu.make_async_copy(p3, par_ref.at[1], sems.at[4]),
    ]
    for copy in copies:
        copy.start()
    for copy in copies:
        copy.wait()
    rows = parts3(in_ref[0]) + parts3(in_ref[1]) + [jnp.zeros((10, 128), jnp.float32)]
    held_ref[TAPROWS:, :] = jnp.concatenate(rows, axis=0).astype(jnp.bfloat16)
    start = pl.multiple_of(lax.rem(lax.axis_index("row"), 2) * HALF, 16)
    half_ref[...] = held_ref[pl.ds(start, HALF), :]


def first_rows(g_ref, f):
    return ((0, g_ref[4 * f, :, :170]), (176, g_ref[4 * f, :, 170:255]), (261, g_ref[4 * f + 1, :, :85]))


def last_rows(g_ref, f):
    return ((0, g_ref[4 * f + 2, :, 170:255]), (85, g_ref[4 * f + 3, :, :85]), (176, g_ref[4 * f + 3, :, 85:255]))


def write_edge(rows, g_ref, out_ref):
    for f in range(FRAMES):
        for lane, v in rows(g_ref, f):
            out_ref[16 * f : 16 * f + 16, lane : lane + v.shape[1]] = v


def k1t(g_ref, next_ref, mate_ref):
    next_ref[...] = jnp.zeros_like(next_ref)
    mate_ref[...] = jnp.zeros_like(mate_ref)
    core = lax.rem(lax.axis_index("row"), 2)

    @pl.when(core == 0)
    def _():
        write_edge(first_rows, g_ref, next_ref)
        write_edge(last_rows, g_ref, mate_ref)

    @pl.when(core == 1)
    def _():
        write_edge(last_rows, g_ref, next_ref)
        write_edge(first_rows, g_ref, mate_ref)


def k1i(g_ref, held_ref, side_ref, x_ref, mid_ref, acc_ref):
    x_ref[...] = jnp.zeros_like(x_ref)
    plan = (
        ((0, 0, 170),),
        ((0, 170, 255), (1, 0, 85)),
        ((1, 85, 255),),
        ((2, 0, 170),),
        ((2, 170, 255), (3, 0, 85)),
        ((3, 85, 255),),
    )
    for f in range(FRAMES):
        at = slice(16 * f, 16 * f + 16)
        for row, parts in enumerate(plan):
            lane = LEAD + STRIDE * (row + 2)
            for j, lo, hi in parts:
                x_ref[at, lane : lane + hi - lo] = g_ref[4 * f + j, :, lo:hi]
                lane += hi - lo
    mid_ref[: 2 * TAPS, :] = jnp.zeros((2 * TAPS, MID[1]), jnp.bfloat16)
    patches(x_ref, mid_ref, 0, *MID)
    weight = jnp.concatenate([held_ref[:TAPROWS], side_ref[:TAPROWS]], axis=1)
    pilot, s1, s2 = moments(weight, ((mid_ref, 0, *MID),))
    acc_ref[0:8] = s1
    acc_ref[8:16] = s2
    acc_ref[16:24] = jnp.broadcast_to(pilot, (8, 256))


def k1w(x_in_ref, side_ref, far_ref, next_ref, mate_ref, both_ref, x_ref):
    both_ref[:HELD] = side_ref[...]
    both_ref[HELD:] = far_ref[...]
    x_ref[...] = x_in_ref[...]
    core = lax.rem(lax.axis_index("row"), 2)

    def edges(above_ref, below_ref):
        x_ref[:, LEAD : LEAD + 2 * STRIDE] = above_ref[:, : 2 * STRIDE]
        x_ref[:, LEAD + 8 * STRIDE : LEAD + 10 * STRIDE] = below_ref[:, : 2 * STRIDE]

    @pl.when(core == 0)
    def _():
        edges(next_ref, mate_ref)

    @pl.when(core == 1)
    def _():
        edges(mate_ref, next_ref)


def patches(x_ref, out_ref, lane, lo, size):
    for f in range(FRAMES):
        for b in range(3):
            for e in range(3):
                at = (f + 2) * TAPS + (3 * b + e) * 16
                start = LEAD + lo + STRIDE * b + e - 1
                out_ref[at : at + 16, lane : lane + size] = x_ref[16 * f : 16 * f + 16, start : start + size]


def valid(lo, size):
    at = lo + lax.broadcasted_iota(jnp.int32, (size, 128), 0)
    ok = (at >= STRIDE) & (at < STRIDE + OWN)
    for row in range(1, 7):
        gap = STRIDE * row + W
        if lo < gap + STRIDE - W and gap < lo + size:
            ok = ok & ((at < gap) | (at >= gap + STRIDE - W))
    return ok


def moments(weight, chunks, carry=None):
    lanes = weight.shape[1]
    zero = jnp.zeros((8, lanes), jnp.float32)
    pilot, s1, s2 = carry or (None, zero, zero)
    for g in range(FRAMES):
        for ref, lane, lo, size in chunks:
            h = lax.dot_general(
                ref[max(g, 2) * TAPS : (g + 3) * TAPS, lane : lane + size],
                weight[max(2 - g, 0) * TAPS :],
                (((0,), (0,)), ((), ())),
                preferred_element_type=jnp.float32,
            )
            ok = jnp.concatenate([valid(lo, size)] * (lanes // 128), axis=1)
            if pilot is None:
                cells = sum(lo <= STRIDE * row + col < lo + size for row in range(1, 7) for col in range(W))
                pilot = jnp.sum(jnp.where(ok, h, 0.0), axis=0, keepdims=True) * (1.0 / cells)
            d = jnp.where(ok, h - pilot, 0.0).reshape(size // 8, 8, lanes)
            s1 = s1 + jnp.sum(d, axis=0)
            s2 = s2 + jnp.sum(d * d, axis=0)
    return pilot, s1, s2


def centred(pilot, s1, s2):
    s1 = jnp.sum(s1, axis=0, keepdims=True)
    s2 = jnp.sum(s2, axis=0, keepdims=True)
    d = s1 / (FRAMES * CELLS)
    return pilot + d, s2 - s1 * d


def outer(ref):
    return ((ref, 128, 128, 256), (ref, SIDES, SPAN - SIDES, 256))


def k1p(x_ref, held_ref, side_ref, acc_ref, out_ref, near_ref):
    out_ref[: 2 * TAPS, :] = jnp.zeros((2 * TAPS, 2 * SIDES), jnp.bfloat16)
    patches(x_ref, out_ref, 0, 0, SIDES)
    patches(x_ref, out_ref, SIDES, SPAN - SIDES, SIDES)
    weight = jnp.concatenate([held_ref[:TAPROWS], side_ref[:TAPROWS]], axis=1)
    mean, squares = centred(*moments(weight, outer(out_ref), (acc_ref[16:17], acc_ref[0:8], acc_ref[8:16])))
    for i in range(2):
        near_ref[i : i + 1] = mean[:, 128 * i : 128 * (i + 1)]
        near_ref[2 + i : 3 + i] = squares[:, 128 * i : 128 * (i + 1)]
    near_ref[4:] = jnp.zeros((4, 128), jnp.float32)


def k1q(mid_ref, out_ref, near_ref, held_ref, mine_ref, other_ref, wall_ref, st_ref):
    c, core = lax.axis_index("ch"), lax.rem(lax.axis_index("row"), 2)
    up = jnp.where((lax.axis_index("row") >= 8) == (core == 0), 1, 3)
    side, side_x, far = (lax.rem(c + i, 4) for i in (up, 4 - up, 2))
    wall_ref[c] = held_ref[...]
    wall_ref[side] = mine_ref[:HELD, :]
    wall_ref[side_x] = other_ref[:HELD, :]
    wall_ref[far, pl.ds(pl.multiple_of(core * HALF, 16), HALF), :] = mine_ref[HELD:, :]
    wall_ref[far, pl.ds(pl.multiple_of((1 - core) * HALF, 16), HALF), :] = other_ref[HELD:, :]
    weight = jnp.concatenate([other_ref[:TAPROWS], wall_ref[far][:TAPROWS]], axis=1)
    mean, squares = centred(*moments(weight, ((mid_ref, 0, *MID), *outer(out_ref))))

    def send(at, v):
        st_ref[:, pl.ds(at, 1), :] = jnp.broadcast_to(v[None], (16, 1, 128))

    for at, m, q in (
        (c, near_ref[0:1], near_ref[2:3]),
        (side, near_ref[1:2], near_ref[3:4]),
        (side_x, mean[:, :128], squares[:, :128]),
        (far, mean[:, 128:], squares[:, 128:]),
    ):
        send(at, m)
        send(4 + at, q)


def k2(mid_ref, out_ref, wall_ref, st_ref, w2_hbm, mix_ref, so_ref, a_ref, w2_ref, y_ref, sem):
    copy = pltpu.make_async_copy(w2_hbm, w2_ref, sem)
    copy.start()
    f, r = lax.axis_index("frm"), lax.axis_index("row")
    weight = jnp.concatenate([wall_ref[j, :TAPROWS, :] for j in range(4)], axis=1)

    def spread3(at):
        rows = [wall_ref[j, TAPROWS:, :].astype(jnp.float32)[at : at + 3] for j in range(4)]
        return jnp.concatenate([jnp.sum(r, axis=0, keepdims=True) for r in rows], axis=1)

    n = FRAMES * CELLS
    st = st_ref[...]
    sums = jnp.sum(st, axis=0)
    means = sums[:4] * (1.0 / 16)
    off = st[:, :4, :] - means[None]
    spread = jnp.sum(off * off, axis=0)
    mean, var = group_moments(eight(means), eight((sums[4:] * (1.0 / n) + spread) * (1.0 / 16)))
    inverse = lax.rsqrt(var + EPSILON)

    def wide(v):
        return jnp.concatenate([v[j : j + 1] for j in range(4)], axis=1)

    mean, scale, shift = wide(mean), 0.5 * wide(inverse) * spread3(0), 0.5 * spread3(3)

    a_ref[0:16, :] = jnp.zeros((16, 3 * CH), jnp.bfloat16)
    a_ref[16 + SPAN :, :] = jnp.zeros((16, 3 * CH), jnp.bfloat16)
    for k in range(3):
        g = f - 2 + k

        @pl.when(g >= 0)
        def _():
            at = pl.multiple_of(g * TAPS, 16)
            for ref, lane, lo, size in (
                (out_ref, 0, 0, SIDES),
                (mid_ref, 0, *MID),
                (out_ref, SIDES, SPAN - SIDES, SIDES),
            ):
                h = lax.dot_general(
                    ref[pl.ds(at, 3 * TAPS), lane : lane + size],
                    weight,
                    (((0,), (0,)), ((), ())),
                    preferred_element_type=jnp.float32,
                )
                u = silu_of_twice((h - mean) * scale + shift)
                a_ref[16 + lo : 16 + lo + size, k * CH : (k + 1) * CH] = u.astype(jnp.bfloat16)

        @pl.when(g < 0)
        def _():
            a_ref[16 : 16 + SPAN, k * CH : (k + 1) * CH] = jnp.zeros((SPAN, CH), jnp.bfloat16)

    keep = lax.broadcasted_iota(jnp.int32, (16, 3 * CH), 0) < 10
    for row in range(8):
        at = 16 + STRIDE * row + 160
        a_ref[at : at + 16, :] = jnp.where(keep, a_ref[at : at + 16, :], 0).astype(jnp.bfloat16)

    @pl.when(r == 0)
    def _():
        a_ref[16 : 16 + STRIDE, :] = jnp.zeros((STRIDE, 3 * CH), jnp.bfloat16)

    @pl.when(r == 15)
    def _():
        a_ref[16 + 7 * STRIDE : 16 + SPAN, :] = jnp.zeros((STRIDE, 3 * CH), jnp.bfloat16)

    copy.wait()

    def product(start, rows, *taps):
        kernel = jnp.concatenate(
            [jnp.concatenate([w2_ref[9 * a + 3 * b + e] for a in range(3)], axis=0) for b, e in taps], axis=1
        )
        y_ref[:rows, : 128 * len(taps)] = jnp.dot(
            a_ref[start : start + rows, :], kernel, preferred_element_type=jnp.float32
        )

    for b in range(3):
        product(STRIDE * b, OWN + 32, (b, 0), (b, 2))
        part = y_ref[15 : 15 + OWN, :128] + y_ref[17 : 17 + OWN, 128:]
        mix_ref[...] = part if b == 0 else mix_ref[...] + part
    product(16, OWN + STRIDE, (0, 1), (1, 1))
    mix_ref[...] += y_ref[0:OWN, :128] + y_ref[STRIDE : STRIDE + OWN, 128:]
    product(16 + 2 * STRIDE, OWN, (2, 1))
    v = (mix_ref[...] + y_ref[0:OWN, :128]).reshape(ROWS, STRIDE, 128)
    mix_ref[...] = v.reshape(OWN, 128)
    ok = lax.broadcasted_iota(jnp.int32, (ROWS, STRIDE, 128), 1) < W
    total = jnp.sum(jnp.sum(jnp.where(ok, v, 0.0), axis=0), axis=0, keepdims=True)
    centre = total / CELLS
    off = jnp.where(ok, v - centre[None], 0.0)
    squares = jnp.sum(jnp.sum(off * off, axis=0), axis=0, keepdims=True)
    so_ref[:, 0:1, :] = jnp.broadcast_to(centre[None], (64, 1, 128))
    so_ref[:, 1:2, :] = jnp.broadcast_to(squares[None], (64, 1, 128))


def k3(mix_ref, st_ref, par_ref, out_ref):
    st = st_ref[...]
    sums = jnp.sum(st, axis=0)
    means = sums * (1.0 / 64)
    off = st - means[None]
    spread = jnp.sum(off * off, axis=0)
    var = (sums[1:2] * (1.0 / CELLS) + spread[0:1]) * (1.0 / 64)
    mean, var = group_moments(eight(means[0:1]), eight(var))
    mean = mean[:1]
    scale = 0.5 * lax.rsqrt(var[:1] + EPSILON) * par_ref[0]
    shift = 0.5 * par_ref[1]
    for row in range(ROWS):
        v = mix_ref[STRIDE * row : STRIDE * (row + 1), :]
        u = silu_of_twice((v - mean) * scale + shift)
        out_ref[0, row] = u[:W].astype(jnp.bfloat16)


def shape(dims, kind):
    return jax.ShapeDtypeStruct(dims, kind)


INHBM = pl.BlockSpec(memory_space=pltpu.HBM)
INVMEM = pl.BlockSpec(memory_space=pltpu.VMEM)


def in_hbm(v):
    return pltpu.with_memory_space_constraint(v, pltpu.HBM)


def call_k0(tokens):
    return pl.pallas_call(
        k0,
        out_shape=shape((16, C_LAT, 255), jnp.bfloat16),
        in_specs=[INHBM],
        out_specs=INVMEM,
        scratch_shapes=[pltpu.VMEM((C_LAT, 255), jnp.bfloat16), pltpu.SemaphoreType.DMA],
        compiler_params=pltpu.CompilerParams(vmem_limit_bytes=VMEM),
        name="k0",
    )(in_hbm(tokens))


def call_k0w(*arrays):
    return pl.pallas_call(
        k0w,
        out_shape=(
            shape((HELD, 128), jnp.bfloat16),
            shape((HALF, 128), jnp.bfloat16),
            shape((2, 1, 128), jnp.float32),
        ),
        in_specs=[INHBM] * 5,
        out_specs=(INVMEM,) * 3,
        scratch_shapes=[pltpu.VMEM((2, 1, 128), jnp.float32), pltpu.SemaphoreType.DMA((5,))],
        compiler_params=pltpu.CompilerParams(vmem_limit_bytes=VMEM),
        name="k0w",
    )(*[in_hbm(v) for v in arrays])


def call(kernel, name, outs, *arrays):
    return pl.pallas_call(
        kernel,
        out_shape=tuple(shape(*out) for out in outs),
        in_specs=[INVMEM] * len(arrays),
        out_specs=(INVMEM,) * len(outs),
        compiler_params=pltpu.CompilerParams(vmem_limit_bytes=VMEM),
        name=name,
    )(*arrays)


def call_k2(*arrays):
    return pl.pallas_call(
        k2,
        out_shape=(shape((OWN, 128), jnp.float32), shape((64, 2, 128), jnp.float32)),
        in_specs=[INVMEM] * 4 + [INHBM],
        out_specs=(INVMEM,) * 2,
        scratch_shapes=[
            pltpu.VMEM((SPAN + 32, 3 * CH), jnp.bfloat16),
            pltpu.VMEM((27, CH, 128), jnp.bfloat16),
            pltpu.VMEM((SPAN, 256), jnp.float32),
            pltpu.SemaphoreType.DMA,
        ],
        compiler_params=pltpu.CompilerParams(vmem_limit_bytes=VMEM),
        name="k2",
    )(*arrays[:4], in_hbm(arrays[4]))


def call_k3(mix, st, par):
    return pl.pallas_call(
        k3,
        out_shape=shape((1, ROWS, W, 128), jnp.bfloat16),
        in_specs=[INVMEM] * 3,
        out_specs=INVMEM,
        compiler_params=pltpu.CompilerParams(vmem_limit_bytes=VMEM),
        name="k3",
    )(mix, st, par)


def per_device(latents, in_weight, in_gain, in_shift, mid_weight, mid_gain, mid_shift):
    params = [v.reshape(1, 128) for v in (in_gain, in_shift, mid_gain, mid_shift)]
    g = lax.all_to_all(call_k0(latents.T), ("frm", "ch"), 0, 0)
    held, half, par = call_k0w(in_weight.reshape(TAPROWS, 128), *params)
    sides = []
    for i in range(16):
        zl, core = i // 8, i % 2
        for j in range(4):
            up = (zl == 0) if core else (zl == 1)
            source = i if core else i ^ 8
            sides.append((4 * source + (j + (1 if up else 3)) % 4, 4 * i + j))
    side = lax.ppermute(held, ("row", "ch"), sides)
    fars = [(4 * (i ^ 8) + (j + 2) % 4, 4 * i + j) for i in range(16) for j in range(4)]
    far = lax.ppermute(half, ("row", "ch"), fars)
    cores = [(i, i ^ 1) for i in range(16)]
    edge = ((16 * FRAMES, 384), jnp.bfloat16)
    to_next, to_mate = call(k1t, "k1t", [edge] * 2, g)
    to_next = lax.ppermute(to_next, "row", [(i, i + 2 * (i % 2) - 1) for i in range(1, 15)])
    to_mate = lax.ppermute(to_mate, "row", cores)
    own = ((16 * FRAMES, XLANES), jnp.bfloat16)
    outs = [own, ((6 * TAPS, MID[1]), jnp.bfloat16), ((24, 256), jnp.float32)]
    x, mid, acc = call(k1i, "k1i", outs, g, held, side)
    mine, x = call(k1w, "k1w", [((HELD + HALF, 128), jnp.bfloat16), own], x, side, far, to_next, to_mate)
    other = lax.ppermute(mine, "row", cores)
    outs = [((6 * TAPS, 2 * SIDES), jnp.bfloat16), ((8, 128), jnp.float32)]
    outer_patches, near = call(k1p, "k1p", outs, x, held, side, acc)
    outs = [((4, HELD, 128), jnp.bfloat16), ((16, 8, 128), jnp.float32)]
    wall, st = call(k1q, "k1q", outs, mid, outer_patches, near, held, mine, other)
    st = lax.all_to_all(st, "row", 0, 0)
    mix, st = call_k2(mid, outer_patches, wall, st, mid_weight)
    st = lax.all_to_all(st, ("frm", "row"), 0, 0)
    return call_k3(mix, st, par)


def solution(mesh):
    return jax.shard_map(
        per_device,
        mesh=mesh,
        in_specs=(
            P(("frm", "row", "ch"), None),
            P(None, None, "ch"),
            P("ch"),
            P("ch"),
            P(None, None, "ch"),
            P("ch"),
            P("ch"),
        ),
        out_specs=P("frm", "row", None, "ch"),
        check_vma=False,
    )
```
